32 devices in a mesh: groups: 2 (over y), space: 4 (over z), dp: 2 (over x), chan: 2 (over core).
Axes of the slice: x: 2, y: 2, z: 4, core: 2. Of those that a mesh axis runs over, the one named last changes fastest.
Arguments:
- grid: bfloat16 [4, 1024, 512], P(('groups', 'dp'), 'space'), parts along dimension 0, may hold values from -6 to 6
- mesh_nodes: bfloat16 [4, 512, 512], P(('groups', 'dp'), 'space'), parts along dimension 0, may hold values from -6 to 6
- cot: bfloat16 [4, 512, 512], P(('groups', 'dp'), 'space'), parts along dimension 0, may hold values from -6 to 6
- enc_send: bfloat16 [512, 512], P(None, 'chan'), may hold values from -0.25 to 0.25
- enc_recv: bfloat16 [512, 512], P(None, 'chan'), may hold values from -0.25 to 0.25
- enc_out: bfloat16 [512, 512], P('chan'), may hold values from -0.25 to 0.25
- proc_send: bfloat16 [512, 512], P(None, 'chan'), may hold values from -0.25 to 0.25
- proc_recv: bfloat16 [512, 512], P(None, 'chan'), may hold values from -0.25 to 0.25
- proc_out: bfloat16 [512, 512], P('chan'), may hold values from -0.25 to 0.25
- enc_sender: int32 [2048], P('space'), may hold values from 0 to 1023, as said below
- enc_receiver: int32 [2048], P('space'), may hold values from 0 to 511, as said below
- enc_count: int32 [4], P('space'), may hold values from 256 to 512, as said below
- proc_sender: int32 [2048], P('space'), may hold values from 0 to 511, as said below
- proc_receiver: int32 [2048], P('space'), may hold values from 0 to 511, as said below
- proc_count: int32 [4], P('space'), may hold values from 256 to 512, as said below
Outputs:
- mesh_out: bfloat16 [4, 512, 512], P(('groups', 'dp'), 'space'), parts along dimension 0
- grid_grad: float32 [4, 1024, 512], P(('groups', 'dp'), 'space'), parts along dimension 0
- mesh_grad: float32 [4, 512, 512], P(('groups', 'dp'), 'space'), parts along dimension 0
- enc_send_grad: float32 [1024, 512], P(('groups', 'space', 'dp'), 'chan'), parts along dimension 0
- enc_recv_grad: float32 [1024, 512], P(('groups', 'space', 'dp'), 'chan'), parts along dimension 0
- enc_out_grad: float32 [1024, 512], P(('groups', 'chan'), ('space', 'dp')), parts along dimension 0
- proc_send_grad: float32 [1024, 512], P(('groups', 'space', 'dp'), 'chan'), parts along dimension 0
- proc_recv_grad: float32 [1024, 512], P(('groups', 'space', 'dp'), 'chan'), parts along dimension 0
- proc_out_grad: float32 [1024, 512], P(('groups', 'chan'), ('space', 'dp')), parts along dimension 0
The draws below stay inside these ranges and needn't reach their ends.
There are 2 independent parts, one for each index of `groups`. The reference program is written for one: setup_inputs(seed, part) draws one part's arguments, and reference() takes and returns one part's arrays. A program takes and returns all parts, laid end to end along the dimension named above; an argument that names none is the same for every part. Nothing has to cross between parts.
Inputs may be any that keep to these rules, and one draw needn't show every extreme that they name: `enc_sender`: grid nodes are numbered region by region, 256 to a region; block k holds slots k * 512 to (k + 1) * 512 - 1. In every block, padded slots included, at most 16 slots name senders of any one other region, and some other region supplies exactly 16. `enc_receiver`: mesh nodes are numbered region by region, 128 to a region; every slot of block k names a mesh node of region k. The first enc_count[k] slots of block k are live, the rest padding; some block is full. `proc_sender`: block k holds slots k * 512 to (k + 1) * 512 - 1. In every block, padded slots included, at most 16 slots name senders of any one other region, and some other region supplies exactly 16. `proc_receiver`: every slot of block k names a mesh node of region k. The first proc_count[k] slots of block k are live, the rest padding; some block is full.
All inputs are finite; a program needn't handle non-finite values.
Results may differ from the reference program's by a relative error of at most 0.0062.
Values may be sent and summed in bfloat16 or wider, within the bound.
A program may use at most 64 MiB of HBM per device.

```python
import jax
import jax.numpy as jnp
from jax import lax

H = 512
F = 512
G_DEV = 256
M_DEV = 128
E_ENC = 512
E_PROC = 512
CAP = 16
B = 2
NG = 1024
NM = 512
N_SPACE = 4


def region_senders(key, node_total, slot_total, bound):
    key_peer, key_coin, key_local, key_shuffle = jax.random.split(key, 4)
    regions = N_SPACE
    peer_total = min(14, regions - 1)
    scores = jax.random.randint(key_peer, (regions, regions - 1), 0, 2 ** 20) * regions + jnp.arange(regions - 1)[None, :]
    offsets = jnp.argsort(scores, axis=1)[:, :peer_total] + 1
    peers = (jnp.arange(regions)[:, None] + offsets) % regions
    slot_index = jnp.arange(slot_total)
    section = jnp.minimum(slot_index // bound, peer_total)
    coin_flip = jax.random.randint(key_coin, (regions, slot_total), 0, 8)
    remote = (section == 0)[None, :] | (section < peer_total)[None, :] & (coin_flip < 7)
    chosen = jnp.take_along_axis(peers, jnp.broadcast_to(jnp.minimum(section, peer_total - 1)[None, :], (regions, slot_total)), axis=1)
    owners = jnp.where(remote, chosen, jnp.arange(regions)[:, None])
    local_row = jax.random.randint(key_local, (regions, slot_total), 0, node_total)
    names = owners * node_total + local_row
    shuffle = jnp.argsort(jax.random.randint(key_shuffle, (regions, slot_total), 0, 2 ** 16) * slot_total + slot_index[None, :], axis=1)
    return jnp.take_along_axis(names, shuffle, axis=1).reshape(-1).astype(jnp.int32)


def region_receivers(key, node_total, slot_total):
    local_row = jax.random.randint(key, (N_SPACE, slot_total), 0, node_total)
    return (jnp.arange(N_SPACE)[:, None] * node_total + local_row).reshape(-1).astype(jnp.int32)


def block_counts(key, slot_total):
    key_count, key_full = jax.random.split(key)
    counts = jax.random.randint(key_count, (N_SPACE,), slot_total // 2, slot_total + 1)
    full_block = jax.random.randint(key_full, (), 0, N_SPACE)
    return jnp.where(jnp.arange(N_SPACE) == full_block, slot_total, counts).astype(jnp.int32)


def draw_enc_sender(key, part):
    key = jax.random.fold_in(key, 11)
    return region_senders(key, G_DEV, E_ENC, CAP)


def draw_enc_receiver(key, part):
    key = jax.random.fold_in(key, 12)
    return region_receivers(key, M_DEV, E_ENC)


def draw_enc_count(key, part):
    key = jax.random.fold_in(key, 13)
    return block_counts(key, E_ENC)


def draw_proc_sender(key, part):
    key = jax.random.fold_in(key, 14)
    return region_senders(key, M_DEV, E_PROC, CAP)


def draw_proc_receiver(key, part):
    key = jax.random.fold_in(key, 15)
    return region_receivers(key, M_DEV, E_PROC)


def draw_proc_count(key, part):
    key = jax.random.fold_in(key, 16)
    return block_counts(key, E_PROC)


def steps_of(stream_key, shape, cuts, least, high):
    factor_of = 1.0
    for position, shards_of in cuts:
        draws = jax.random.uniform(jax.random.fold_in(jax.random.fold_in(stream_key, 6), position), (shards_of,), jnp.float32, least / len(cuts), high / len(cuts))
        factor_of = factor_of * jnp.repeat(jnp.exp(draws), shape[position] // shards_of).reshape((-1,) + (1,) * (len(shape) - 1 - position))
    return factor_of


def scatter_about(stream_key, dims, width, limit, cuts=(), kind=jnp.bfloat16):
    values = jax.random.normal(stream_key, dims, jnp.float32) * width
    if len(cuts) > 0:
        values = steps_of(stream_key, dims, cuts, -0.22, 0.18) * values
    return jnp.clip(values, min=-limit, max=limit).astype(kind)


def setup_inputs(seed: int = 0, part: int = 0) -> dict:
    keys = jax.random.split(jax.random.key(seed), 16)
    part_splits = jax.random.split(jax.random.fold_in(keys[15], part), 16)
    grid = scatter_about(part_splits[0], (B, NG, H), 1.0, 6.0, ((0, 2), (1, 4)))
    mesh_nodes = scatter_about(part_splits[1], (B, NM, H), 1.0, 6.0, ((0, 2), (1, 4)))
    cot = scatter_about(part_splits[2], (B, NM, H), 1.0, 6.0, ((0, 2), (1, 4)))
    enc_send = scatter_about(keys[3], (H, F), H ** -0.5, 0.25, ((1, 2),))
    enc_recv = scatter_about(keys[4], (H, F), H ** -0.5, 0.25, ((1, 2),))
    enc_out = scatter_about(keys[5], (F, H), F ** -0.5, 0.25, ((0, 2),))
    proc_send = scatter_about(keys[6], (H, F), H ** -0.5, 0.25, ((1, 2),))
    proc_recv = scatter_about(keys[7], (H, F), H ** -0.5, 0.25, ((1, 2),))
    proc_out = scatter_about(keys[8], (F, H), F ** -0.5, 0.25, ((0, 2),))
    enc_sender = draw_enc_sender(jax.random.fold_in(keys[15], 71), part)
    enc_receiver = draw_enc_receiver(jax.random.fold_in(keys[15], 71), part)
    enc_count = draw_enc_count(jax.random.fold_in(keys[15], 71), part)
    proc_sender = draw_proc_sender(jax.random.fold_in(keys[15], 71), part)
    proc_receiver = draw_proc_receiver(jax.random.fold_in(keys[15], 71), part)
    proc_count = draw_proc_count(jax.random.fold_in(keys[15], 71), part)
    return {"grid": grid, "mesh_nodes": mesh_nodes, "cot": cot, "enc_send": enc_send, "enc_recv": enc_recv, "enc_out": enc_out, "proc_send": proc_send, "proc_recv": proc_recv, "proc_out": proc_out, "enc_sender": enc_sender, "enc_receiver": enc_receiver, "enc_count": enc_count, "proc_sender": proc_sender, "proc_receiver": proc_receiver, "proc_count": proc_count}


def times_transposed(left, right):
    return lax.dot_general(left, right, (((1,), (1,)), ((), ())), preferred_element_type=jnp.float32)


def left_transposed(left, right):
    return lax.dot_general(left, right, (((0,), (0,)), ((), ())), preferred_element_type=jnp.float32)


def live_slots(counts, per_block):
    slot_index = jnp.arange(counts.shape[0] * per_block, dtype=jnp.int32)
    return (slot_index % per_block) < jnp.repeat(counts, per_block)


def edge_forward(sender_rows, receiver_rows, w_send, w_recv, w_out, live):
    preact = jnp.dot(sender_rows, w_send, preferred_element_type=jnp.float32) + jnp.dot(receiver_rows, w_recv, preferred_element_type=jnp.float32)
    gate_value = jax.nn.sigmoid(preact)
    activation = (preact * gate_value).astype(jnp.bfloat16)
    message = jnp.where(live[:, None], jnp.dot(activation, w_out, preferred_element_type=jnp.float32), jnp.zeros((), jnp.float32))
    return preact, gate_value, activation, message


def edge_backward(message_grad, preact, gate_value, w_out):
    hidden_grad = times_transposed(message_grad, w_out)
    return (hidden_grad * gate_value * (1.0 + preact * (1.0 - gate_value))).astype(jnp.bfloat16)


def reference(grid, mesh_nodes, cot, enc_send, enc_recv, enc_out, proc_send, proc_recv, proc_out, enc_sender, enc_receiver, enc_count, proc_sender, proc_receiver, proc_count):
    enc_live = live_slots(enc_count, E_ENC)
    proc_live = live_slots(proc_count, E_PROC)
    outputs, grid_grads, mesh_grads = [], [], []
    weight_sums = [jnp.zeros((H, F), jnp.float32), jnp.zeros((H, F), jnp.float32), jnp.zeros((F, H), jnp.float32), jnp.zeros((H, F), jnp.float32), jnp.zeros((H, F), jnp.float32), jnp.zeros((F, H), jnp.float32)]
    for sample in range(B):
        grid_rows = grid[sample]
        mesh_rows = mesh_nodes[sample]
        cot_rows = cot[sample]
        enc_senders = jnp.take(grid_rows, enc_sender, axis=0)
        enc_receivers = jnp.take(mesh_rows, enc_receiver, axis=0)
        enc_pre, enc_gate, enc_act, enc_msg = edge_forward(enc_senders, enc_receivers, enc_send, enc_recv, enc_out, enc_live)
        enc_sum = jax.ops.segment_sum(enc_msg, enc_receiver, num_segments=NM)
        mesh_mid = (mesh_rows.astype(jnp.float32) + enc_sum).astype(jnp.bfloat16)
        proc_senders = jnp.take(mesh_mid, proc_sender, axis=0)
        proc_receivers = jnp.take(mesh_mid, proc_receiver, axis=0)
        proc_pre, proc_gate, proc_act, proc_msg = edge_forward(proc_senders, proc_receivers, proc_send, proc_recv, proc_out, proc_live)
        proc_sum = jax.ops.segment_sum(proc_msg, proc_receiver, num_segments=NM)
        outputs.append((mesh_mid.astype(jnp.float32) + proc_sum).astype(jnp.bfloat16))
        proc_dmsg = jnp.where(proc_live[:, None], jnp.take(cot_rows, proc_receiver, axis=0), jnp.zeros((), jnp.bfloat16))
        proc_dpre = edge_backward(proc_dmsg, proc_pre, proc_gate, proc_out)
        weight_sums[5] = weight_sums[5] + left_transposed(proc_act, proc_dmsg)
        weight_sums[3] = weight_sums[3] + left_transposed(proc_senders, proc_dpre)
        weight_sums[4] = weight_sums[4] + left_transposed(proc_receivers, proc_dpre)
        into_receivers = jax.ops.segment_sum(times_transposed(proc_dpre, proc_recv), proc_receiver, num_segments=NM)
        into_senders = jax.ops.segment_sum(times_transposed(proc_dpre, proc_send), proc_sender, num_segments=NM)
        mesh_mid_grad = cot_rows.astype(jnp.float32) + (into_receivers + into_senders)
        enc_dmsg = jnp.where(enc_live[:, None], jnp.take(mesh_mid_grad.astype(jnp.bfloat16), enc_receiver, axis=0), jnp.zeros((), jnp.bfloat16))
        enc_dpre = edge_backward(enc_dmsg, enc_pre, enc_gate, enc_out)
        weight_sums[2] = weight_sums[2] + left_transposed(enc_act, enc_dmsg)
        weight_sums[0] = weight_sums[0] + left_transposed(enc_senders, enc_dpre)
        weight_sums[1] = weight_sums[1] + left_transposed(enc_receivers, enc_dpre)
        grid_grads.append(jax.ops.segment_sum(times_transposed(enc_dpre, enc_send), enc_sender, num_segments=NG))
        mesh_grads.append(mesh_mid_grad + jax.ops.segment_sum(times_transposed(enc_dpre, enc_recv), enc_receiver, num_segments=NM))
    return (jnp.stack(outputs), jnp.stack(grid_grads), jnp.stack(mesh_grads), weight_sums[0], weight_sums[1], weight_sums[2], weight_sums[3], weight_sums[4], weight_sums[5])
```

```python
import functools

import jax
import jax.numpy as jnp
from jax import lax
from jax.experimental import pallas as pl
from jax.experimental.pallas import tpu as pltpu
from jax.sharding import PartitionSpec as P

CAP = 16


def times_transposed(left, right):
    return lax.dot_general(
        left, right, (((1,), (1,)), ((), ())), preferred_element_type=jnp.float32
    )


def left_transposed(left, right):
    return lax.dot_general(
        left, right, (((0,), (0,)), ((), ())), preferred_element_type=jnp.float32
    )


def exact_product(left, right):
    return jnp.dot(left, right, preferred_element_type=jnp.float32, precision=lax.Precision.HIGHEST)


def region_plan(sender, live_count, node_total, regions, own_region, slot_total):
    owners = sender // node_total
    local_row = sender - owners * node_total
    remote = owners != own_region
    edge_total = sender.shape[0]
    live_mask = (jnp.arange(edge_total) < live_count[0]).astype(jnp.float32)
    by_owner = ((owners[:, None] == jnp.arange(regions)[None, :]) & remote[:, None]).astype(
        jnp.int32
    )
    earlier = jnp.cumsum(by_owner, axis=0) - by_owner
    position = jnp.sum(earlier * by_owner, axis=1)
    slot_code = jnp.where(remote, owners * slot_total + position, regions * slot_total)
    requests = (
        jnp.zeros((regions * slot_total,), jnp.int32).at[slot_code].set(local_row + 1, mode="drop")
    )
    lookup = jnp.where(remote, node_total + slot_code, local_row)
    local_scatter = (
        (local_row[None, :] == jnp.arange(node_total)[:, None]) & jnp.logical_not(remote)[None, :]
    ).astype(jnp.float32)
    return (live_mask, slot_code, requests.reshape(regions, slot_total), lookup, local_scatter)


def receiver_scatter(receiver, own_region, node_total):
    local_row = receiver - own_region * node_total
    return (local_row, (local_row[None, :] == jnp.arange(node_total)[:, None]).astype(jnp.float32))


def fetch_rows(block, wanted):
    picked = jnp.take(block, jnp.maximum(wanted - 1, 0), axis=0)
    arrived = lax.all_to_all(picked, "space", split_axis=0, concat_axis=0, tiled=True)
    return jnp.concatenate([block, arrived.reshape(-1, block.shape[1])], axis=0)


def core_total(terms):
    return lax.psum(terms, "chan")


def edge_forward(sender_rows, receiver_rows, w_send, w_recv, w_out, live_mask):
    preact = jnp.dot(sender_rows, w_send, preferred_element_type=jnp.float32) + jnp.dot(
        receiver_rows, w_recv, preferred_element_type=jnp.float32
    )
    gate_value = jax.nn.sigmoid(preact)
    activation = (preact * gate_value).astype(jnp.bfloat16)
    message = jnp.dot(activation, w_out, preferred_element_type=jnp.float32) * live_mask[:, None]
    return (preact, gate_value, activation, message)


def edge_backward(message_grad, preact, gate_value, w_out):
    hidden_grad = times_transposed(message_grad, w_out)
    return (hidden_grad * gate_value * (1.0 + preact * (1.0 - gate_value))).astype(jnp.bfloat16)


def sender_terms(preact_grad, w_send, slot_code, wanted, local_scatter, regions, slot_total):
    input_grad = times_transposed(preact_grad, w_send)
    local_part = exact_product(local_scatter, input_grad)
    outgoing = (
        jnp.zeros((regions * slot_total, input_grad.shape[1]), jnp.float32)
        .at[slot_code]
        .set(input_grad, mode="drop")
    )
    incoming = (
        lax.all_to_all(
            outgoing.reshape(regions, slot_total, -1).astype(jnp.bfloat16),
            "space",
            split_axis=0,
            concat_axis=0,
            tiled=True,
        )
        .astype(jnp.float32)
        .reshape(regions * slot_total, -1)
    )
    node_total = local_scatter.shape[0]
    owner_scatter = (wanted.reshape(-1)[None, :] - 1 == jnp.arange(node_total)[:, None]).astype(
        jnp.float32
    )
    return local_part + exact_product(owner_scatter, incoming)


def body(
    grid,
    mesh_nodes,
    cot,
    enc_send,
    enc_recv,
    enc_out,
    proc_send,
    proc_recv,
    proc_out,
    enc_sender,
    enc_receiver,
    enc_count,
    proc_sender,
    proc_receiver,
    proc_count,
):
    regions = lax.axis_size("space")
    own_region = lax.axis_index("space")
    grid_block = grid[0]
    mesh_block = mesh_nodes[0]
    cot_block = cot[0]
    grid_total = grid_block.shape[0]
    mesh_total = mesh_block.shape[0]
    enc_plan = region_plan(enc_sender, enc_count, grid_total, regions, own_region, CAP)
    proc_plan = region_plan(proc_sender, proc_count, mesh_total, regions, own_region, CAP)
    enc_wanted, proc_wanted = (
        lax.all_to_all(enc_plan[2], "space", split_axis=0, concat_axis=0, tiled=True),
        lax.all_to_all(proc_plan[2], "space", split_axis=0, concat_axis=0, tiled=True),
    )
    enc_local_recv, enc_onehot = receiver_scatter(enc_receiver, own_region, mesh_total)
    proc_local_recv, proc_onehot = receiver_scatter(proc_receiver, own_region, mesh_total)
    enc_table = fetch_rows(grid_block, enc_wanted)
    enc_senders = jnp.take(enc_table, enc_plan[3], axis=0)
    enc_receivers = jnp.take(mesh_block, enc_local_recv, axis=0)
    enc_pre, enc_gate, enc_act, enc_msg = edge_forward(
        enc_senders, enc_receivers, enc_send, enc_recv, enc_out, enc_plan[0]
    )
    enc_summed = core_total(exact_product(enc_onehot, enc_msg))
    mesh_mid = (mesh_block.astype(jnp.float32) + enc_summed).astype(jnp.bfloat16)
    proc_table = fetch_rows(mesh_mid, proc_wanted)
    proc_senders = jnp.take(proc_table, proc_plan[3], axis=0)
    proc_receivers = jnp.take(mesh_mid, proc_local_recv, axis=0)
    proc_pre, proc_gate, proc_act, proc_msg = edge_forward(
        proc_senders, proc_receivers, proc_send, proc_recv, proc_out, proc_plan[0]
    )
    proc_summed = core_total(exact_product(proc_onehot, proc_msg))
    mesh_out = (mesh_mid.astype(jnp.float32) + proc_summed).astype(jnp.bfloat16)
    proc_dmsg = jnp.where(
        proc_plan[0][:, None] > 0,
        jnp.take(cot_block, proc_local_recv, axis=0),
        jnp.zeros((), jnp.bfloat16),
    )
    proc_dpre = edge_backward(proc_dmsg, proc_pre, proc_gate, proc_out)
    proc_out_grad = left_transposed(proc_act, proc_dmsg)
    proc_send_grad = left_transposed(proc_senders, proc_dpre)
    proc_recv_grad = left_transposed(proc_receivers, proc_dpre)
    mesh_part = exact_product(proc_onehot, times_transposed(proc_dpre, proc_recv)) + sender_terms(
        proc_dpre, proc_send, proc_plan[1], proc_wanted, proc_plan[4], regions, CAP
    )
    mesh_mid_grad = cot_block.astype(jnp.float32) + core_total(mesh_part)
    enc_dmsg = jnp.where(
        enc_plan[0][:, None] > 0,
        jnp.take(mesh_mid_grad.astype(jnp.bfloat16), enc_local_recv, axis=0),
        jnp.zeros((), jnp.bfloat16),
    )
    enc_dpre = edge_backward(enc_dmsg, enc_pre, enc_gate, enc_out)
    enc_out_grad = left_transposed(enc_act, enc_dmsg)
    enc_send_grad = left_transposed(enc_senders, enc_dpre)
    enc_recv_grad = left_transposed(enc_receivers, enc_dpre)
    grid_part = sender_terms(enc_dpre, enc_send, enc_plan[1], enc_wanted, enc_plan[4], regions, CAP)
    receiver_part = exact_product(enc_onehot, times_transposed(enc_dpre, enc_recv))
    grid_summed, receiver_summed = core_total((grid_part, receiver_part))
    mesh_grad = mesh_mid_grad + receiver_summed
    shared = (
        lax.psum_scatter(enc_send_grad, ("space", "dp"), scatter_dimension=0, tiled=True),
        lax.psum_scatter(enc_recv_grad, ("space", "dp"), scatter_dimension=0, tiled=True),
        lax.psum_scatter(enc_out_grad, ("space", "dp"), scatter_dimension=1, tiled=True),
        lax.psum_scatter(proc_send_grad, ("space", "dp"), scatter_dimension=0, tiled=True),
        lax.psum_scatter(proc_recv_grad, ("space", "dp"), scatter_dimension=0, tiled=True),
        lax.psum_scatter(proc_out_grad, ("space", "dp"), scatter_dimension=1, tiled=True),
    )
    return (
        mesh_out[None],
        grid_summed[None],
        mesh_grad[None],
        shared[0],
        shared[1],
        shared[2],
        shared[3],
        shared[4],
        shared[5],
    )


F32 = jnp.float32
BF16 = jnp.bfloat16


def dot(left, right):
    return jnp.dot(left, right, preferred_element_type=F32)


def halves(values):
    high = values.astype(BF16)
    return high, (values - high.astype(F32)).astype(BF16)


def dot_split(left, values):
    high, low = halves(values)
    return dot(left, high) + dot(left, low)


def split_dot_transposed(values, right):
    high, low = halves(values)
    return times_transposed(high, right) + times_transposed(low, right)


def split_dot(values, right):
    high, low = halves(values)
    return dot(high, right) + dot(low, right)


def onehot(condition):
    return jnp.where(condition, 1.0, 0.0).astype(BF16)


def iota(shape, dim):
    return lax.broadcasted_iota(jnp.int32, shape, dim).astype(F32)


def fused_kernel(
    regions,
    samples,
    cores,
    grid_ref,
    mesh_ref,
    cot_ref,
    enc_send,
    enc_recv,
    enc_out,
    proc_send,
    proc_recv,
    proc_out,
    enc_sender,
    enc_receiver,
    enc_count,
    proc_sender,
    proc_receiver,
    proc_count,
    mesh_out,
    grid_grad,
    mesh_grad,
    g_enc_send,
    g_enc_recv,
    g_enc_out,
    g_proc_send,
    g_proc_recv,
    g_proc_out,
    req_out,
    req_in,
    row_out,
    row_in,
    term_out,
    term_in,
    part_out,
    part_in,
    last_out,
    last_in,
    full_grad,
    pair_out,
    pair_in,
    ring_own,
    ring_out,
    ring_in,
    send_sem,
    recv_sem,
):
    own = lax.axis_index("space")
    sample = lax.axis_index("dp")
    core = lax.axis_index("chan")
    edges = enc_sender.shape[1]
    grid_total = grid_ref.shape[0]
    mesh_total = mesh_ref.shape[0]
    slots = regions * CAP
    used = [0]

    def space_at(step):
        return lax.rem(own + step, regions)

    def core_at(step):
        return lax.rem(core + step, cores)

    def place(s, d, c):
        return {"space": s, "dp": d, "chan": c}

    def send(src, dst, target):
        index = used[0]
        used[0] += 1
        copy = pltpu.make_async_remote_copy(
            src_ref=src,
            dst_ref=dst,
            send_sem=send_sem.at[index],
            recv_sem=recv_sem.at[index],
            device_id=target,
            device_id_type=pl.DeviceIdType.MESH,
        )
        copy.start()
        return copy

    def arrive(copies):
        for copy in copies:
            copy.wait_recv()

    everything = []
    friends = []
    for c_step in range(cores):
        for s_step in range(regions):
            if c_step or s_step:
                friends.append(place(space_at(s_step), sample, core_at(c_step)))
    for d_step in range(1, samples):
        friends.append(place(own, lax.rem(sample + d_step, samples), core))
    barrier = pltpu.get_barrier_semaphore()
    for friend in friends:
        pl.semaphore_signal(
            barrier, inc=1, device_id=friend, device_id_type=pl.DeviceIdType.MESH
        )

    owner_rows = 16
    before = onehot(iota((edges, edges), 0) < iota((edges, edges), 1))
    owner_id = iota((owner_rows, edges), 0)
    own_id = own.astype(F32)

    def rows_of(sender_ref, receiver_ref, count_ref, total):
        sender = sender_ref[...].astype(F32)
        low = owner_id * total
        owned = (sender >= low) & (sender < low + total)
        local = (sender >= own_id * total) & (sender < own_id * total + total)
        by_owner = jnp.where(owned & (owner_id != own_id), 1.0, 0.0)
        earlier = dot(by_owner.astype(BF16), before)
        code = jnp.sum(by_owner * (owner_id * CAP + earlier), axis=0, keepdims=True)
        owner = jnp.sum(by_owner * owner_id, axis=0, keepdims=True)
        code = jnp.where(local, -1.0, code)
        local_row = jnp.where(local, sender - own_id * total, -1.0)
        wanted = sender - owner * total + 1.0
        receiver = receiver_ref[...].astype(F32) - own_id * mesh_total
        alive = iota((1, edges), 1) < count_ref[...].astype(F32)
        live_receiver = jnp.where(alive, receiver, -1.0)
        match = code == iota((slots, edges), 0)
        request = jnp.sum(jnp.where(match, wanted, 0.0), axis=1, keepdims=True)
        return (local_row, code, receiver, live_receiver), onehot(match), request

    enc_rows, enc_match, enc_request = rows_of(enc_sender, enc_receiver, enc_count, grid_total)
    proc_rows, proc_match, proc_request = rows_of(
        proc_sender, proc_receiver, proc_count, mesh_total
    )
    req_out[:, 0:CAP, :] = jnp.broadcast_to(enc_request, (slots, 128)).reshape(regions, CAP, 128)
    req_out[:, CAP : 2 * CAP, :] = jnp.broadcast_to(proc_request, (slots, 128)).reshape(
        regions, CAP, 128
    )
    req_in[own] = jnp.zeros(req_in.shape[1:], F32)
    for graph in range(2):
        row_in[graph, own] = jnp.zeros(row_in.shape[2:], BF16)
        for c_step in range(cores):
            term_in[graph, c_step, own] = jnp.zeros(term_in.shape[3:], BF16)

    pl.semaphore_wait(barrier, len(friends))
    requests = [
        send(req_out.at[space_at(step)], req_in.at[own], place(space_at(step), sample, core))
        for step in range(1, regions)
    ]
    everything += requests

    columns = jnp.transpose(jnp.concatenate(list(enc_rows) + list(proc_rows), axis=0))

    def tables(rows, first, total):
        by_edge = [columns[:, first + i : first + i + 1] for i in range(4)]
        return (
            onehot(by_edge[0] == iota((edges, total), 1)),
            onehot(by_edge[1] == iota((edges, slots), 1)),
            onehot(by_edge[2] == iota((edges, mesh_total), 1)),
            onehot(by_edge[3] == iota((edges, mesh_total), 1)),
            onehot(rows[0] == iota((total, edges), 0)),
            onehot(rows[2] == iota((mesh_total, edges), 0)),
            onehot(rows[3] == iota((mesh_total, edges), 0)),
        )

    e_pick, e_far, e_recv, e_live, e_pick_t, e_recv_t, e_live_t = tables(
        enc_rows, 0, grid_total
    )
    p_pick, p_far, p_recv, p_live, p_pick_t, p_recv_t, p_live_t = tables(
        proc_rows, 4, mesh_total
    )
    grid_block = grid_ref[...]
    mesh_block = mesh_ref[...]
    cot_block = cot_ref[...]
    enc_pre = dot_split(e_pick, dot(grid_block, enc_send[...])) + dot_split(
        e_recv, dot(mesh_block, enc_recv[...])
    )
    proc_hidden = dot_split(p_live, times_transposed(cot_block, proc_out[...]))

    def picks(graph, total):
        asked = req_in[:, graph * CAP : (graph + 1) * CAP, :].reshape(slots, 128)
        return onehot(asked[:, 0:1] == iota((slots, total), 1) + 1.0)

    def send_rows(graph, pick, block):
        row_out[graph] = dot(pick, block).astype(BF16).reshape(regions, CAP, -1)
        return [
            send(
                row_out.at[graph, space_at(step)],
                row_in.at[graph, own],
                place(space_at(step), sample, core),
            )
            for step in range(1, regions)
        ]

    def far_rows(graph):
        return row_in[graph].reshape(slots, -1)

    arrive(requests)
    enc_asked = picks(0, grid_total)
    rows_sent = send_rows(0, enc_asked, grid_block)
    everything += rows_sent
    proc_asked = picks(1, mesh_total)
    arrive(rows_sent)

    enc_pre = enc_pre + dot_split(e_far, dot(far_rows(0), enc_send[...]))
    enc_gate = jax.nn.sigmoid(enc_pre)
    enc_act_sum = dot(e_live_t, (enc_pre * enc_gate).astype(BF16))
    enc_sum = split_dot(enc_act_sum, enc_out[...])
    other = place(own, sample, core_at(1))
    part_out[0] = enc_sum
    swapped = send(part_out.at[0], part_in.at[0], other)
    everything.append(swapped)
    enc_slope = enc_gate * (1.0 + enc_pre * (1.0 - enc_gate))
    swapped.wait_recv()
    mesh_mid = (mesh_block.astype(F32) + (part_out[0] + part_in[0])).astype(BF16)

    rows_sent = send_rows(1, proc_asked, mesh_mid)
    everything += rows_sent
    proc_pre = dot_split(p_pick, dot(mesh_mid, proc_send[...])) + dot_split(
        p_recv, dot(mesh_mid, proc_recv[...])
    )
    arrive(rows_sent)
    proc_pre = proc_pre + dot_split(p_far, dot(far_rows(1), proc_send[...]))
    proc_gate = jax.nn.sigmoid(proc_pre)
    proc_dpre = (proc_hidden * (proc_gate * (1.0 + proc_pre * (1.0 - proc_gate)))).astype(BF16)

    def send_terms(graph, match, dpre, weights):
        far = dot(match, dpre).astype(BF16)
        term_out[graph] = times_transposed(far, weights).astype(BF16).reshape(regions, CAP, -1)
        copies = []
        for step in range(1, regions):
            for c_step in range(cores):
                copies.append(
                    send(
                        term_out.at[graph, space_at(step)],
                        term_in.at[graph, core, own],
                        place(space_at(step), sample, core_at(c_step)),
                    )
                )
        return far, copies

    def returned(graph, asked):
        return left_transposed(
            jnp.concatenate([asked] * cores, axis=0),
            term_in[graph].reshape(cores * slots, -1),
        )

    proc_far, terms = send_terms(1, proc_match, proc_dpre, proc_send[...])
    everything += terms
    proc_by_sender = dot(p_pick_t, proc_dpre)
    proc_by_receiver = dot(p_recv_t, proc_dpre)
    part_out[1] = split_dot_transposed(proc_by_receiver, proc_recv[...]) + split_dot_transposed(
        proc_by_sender, proc_send[...]
    )
    swapped = send(part_out.at[1], part_in.at[1], other)
    everything.append(swapped)

    shard = full_grad.shape[3]

    def share(index, gradient):
        for s in range(regions):
            for d in range(samples):
                piece = gradient[(s * samples + d) * shard : (s * samples + d + 1) * shard]
                full_grad[index, d, s] = piece
                pair_out[index, d, s] = piece.astype(BF16)
        copies = []
        for step in range(1, samples):
            target = lax.rem(sample + step, samples)
            copies.append(
                send(
                    pair_out.at[index, target],
                    pair_in.at[index, step - 1],
                    place(own, target, core),
                )
            )
        return copies

    def pass_on(index, copies):
        arrive(copies)
        total = full_grad[index, sample]
        for step in range(1, samples):
            total = total + pair_in[index, step - 1].astype(F32)
        ring_own[index] = total
        ring_out[index] = total.astype(BF16)
        return [
            send(
                ring_out.at[index, space_at(step)],
                ring_in.at[index, step - 1],
                place(space_at(step), sample, core),
            )
            for step in range(1, regions)
        ]

    def finish(index, copies):
        arrive(copies)
        total = ring_own[index, own]
        for step in range(1, regions):
            total = total + ring_in[index, step - 1].astype(F32)
        return total

    proc_act_sum = dot(p_live_t, (proc_pre * proc_gate).astype(BF16))
    shared = {}
    shared[5] = share(5, left_transposed(cot_block, proc_act_sum.astype(BF16)))
    shared[3] = share(
        3,
        left_transposed(mesh_mid, proc_by_sender.astype(BF16))
        + left_transposed(far_rows(1), proc_far),
    )
    shared[4] = share(4, left_transposed(mesh_mid, proc_by_receiver.astype(BF16)))
    part_out[2] = split_dot(proc_act_sum, proc_out[...])
    out_swap = send(part_out.at[2], part_in.at[2], other)
    for index in (5, 3, 4):
        everything += shared[index]
    everything.append(out_swap)

    arrive(terms)
    swapped.wait_recv()
    mesh_mid_grad = cot_block.astype(F32) + (
        (part_out[1] + part_in[1]) + returned(1, proc_asked)
    )

    mid_rounded = mesh_mid_grad.astype(BF16)
    enc_hidden = dot_split(e_live, times_transposed(mid_rounded, enc_out[...]))
    enc_dpre = (enc_hidden * enc_slope).astype(BF16)
    shared[2] = share(2, left_transposed(mid_rounded, enc_act_sum.astype(BF16)))
    enc_by_sender = dot(e_pick_t, enc_dpre)
    enc_by_receiver = dot(e_recv_t, enc_dpre)
    enc_far, terms = send_terms(0, enc_match, enc_dpre, enc_send[...])
    shared[0] = share(
        0,
        left_transposed(grid_block, enc_by_sender.astype(BF16))
        + left_transposed(far_rows(0), enc_far),
    )
    shared[1] = share(1, left_transposed(mesh_block, enc_by_receiver.astype(BF16)))
    last_out[0:grid_total] = split_dot_transposed(enc_by_sender, enc_send[...])
    last_out[grid_total : grid_total + mesh_total] = split_dot_transposed(
        enc_by_receiver, enc_recv[...]
    )
    last_swap = send(last_out, last_in, other)
    everything += terms
    for index in (2, 0, 1):
        everything += shared[index]
    everything.append(last_swap)

    passed = {}
    for index in (5, 3, 4, 2, 0, 1):
        passed[index] = pass_on(index, shared[index])
        everything += passed[index]

    out_swap.wait_recv()
    mesh_out[...] = (mesh_mid.astype(F32) + (part_out[2] + part_in[2])).astype(BF16)
    arrive(terms)
    last_swap.wait_recv()
    grid_grad[...] = (last_out[0:grid_total] + last_in[0:grid_total]) + returned(0, enc_asked)
    tail = slice(grid_total, grid_total + mesh_total)
    mesh_grad[...] = mesh_mid_grad + (last_out[tail] + last_in[tail])

    g_proc_out[...] = jnp.transpose(finish(5, passed[5]))
    g_proc_send[...] = finish(3, passed[3])
    g_proc_recv[...] = finish(4, passed[4])
    g_enc_out[...] = jnp.transpose(finish(2, passed[2]))
    g_enc_send[...] = finish(0, passed[0])
    g_enc_recv[...] = finish(1, passed[1])
    for copy in everything:
        copy.wait_send()


def fused_body(regions, samples, cores, grid, mesh_nodes, cot, *rest):
    weights, indices = rest[:6], rest[6:]
    grid_total, width = grid.shape[1:]
    mesh_total = mesh_nodes.shape[1]
    hidden = weights[0].shape[1]
    shard = width // (regions * samples)
    last_total = grid_total + mesh_total
    copies = (regions - 1) * (3 + 2 * cores + 6) + 6 * (samples - 1) + 4
    vmem = pl.BlockSpec(memory_space=pltpu.VMEM)
    outs = pl.pallas_call(
        functools.partial(fused_kernel, regions, samples, cores),
        out_shape=(
            jax.ShapeDtypeStruct((mesh_total, width), BF16),
            jax.ShapeDtypeStruct((grid_total, width), F32),
            jax.ShapeDtypeStruct((mesh_total, width), F32),
            jax.ShapeDtypeStruct((shard, hidden), F32),
            jax.ShapeDtypeStruct((shard, hidden), F32),
            jax.ShapeDtypeStruct((hidden, shard), F32),
            jax.ShapeDtypeStruct((shard, hidden), F32),
            jax.ShapeDtypeStruct((shard, hidden), F32),
            jax.ShapeDtypeStruct((hidden, shard), F32),
        ),
        in_specs=[vmem] * 15,
        out_specs=(vmem,) * 9,
        scratch_shapes=[
            pltpu.VMEM((regions, 2 * CAP, 128), F32),
            pltpu.VMEM((regions, 2 * CAP, 128), F32),
            pltpu.VMEM((2, regions, CAP, width), BF16),
            pltpu.VMEM((2, regions, CAP, width), BF16),
            pltpu.VMEM((2, regions, CAP, width), BF16),
            pltpu.VMEM((2, cores, regions, CAP, width), BF16),
            pltpu.VMEM((3, mesh_total, width), F32),
            pltpu.VMEM((3, mesh_total, width), F32),
            pltpu.VMEM((last_total, width), F32),
            pltpu.VMEM((last_total, width), F32),
            pltpu.VMEM((6, samples, regions, shard, hidden), F32),
            pltpu.VMEM((6, samples, regions, shard, hidden), BF16),
            pltpu.VMEM((6, samples - 1, regions, shard, hidden), BF16),
            pltpu.VMEM((6, regions, shard, hidden), F32),
            pltpu.VMEM((6, regions, shard, hidden), BF16),
            pltpu.VMEM((6, regions - 1, shard, hidden), BF16),
            pltpu.SemaphoreType.DMA((copies,)),
            pltpu.SemaphoreType.DMA((copies,)),
        ],
        compiler_params=pltpu.CompilerParams(
            collective_id=0, has_side_effects=True, vmem_limit_bytes=48 * 2**20
        ),
    )(
        grid[0],
        mesh_nodes[0],
        cot[0],
        *weights,
        *[index.reshape(1, -1) for index in indices],
    )
    return (outs[0][None], outs[1][None], outs[2][None], *outs[3:])


def chosen_body(mesh):
    regions, samples, cores = (mesh.shape[name] for name in ("space", "dp", "chan"))
    shards = regions * samples

    def run(*args):
        width = args[0].shape[2]
        if regions > 16 or samples < 2 or cores != 2 or width % (16 * shards):
            return body(*args)
        return fused_body(regions, samples, cores, *args)

    return run


def solution(mesh):
    placed = (
        P(("groups", "dp"), "space", None),
        P(("groups", "dp"), "space", None),
        P(("groups", "dp"), "space", None),
        P(None, "chan"),
        P(None, "chan"),
        P("chan", None),
        P(None, "chan"),
        P(None, "chan"),
        P("chan", None),
        P("space"),
        P("space"),
        P("space"),
        P("space"),
        P("space"),
        P("space"),
    )
    return jax.shard_map(
        chosen_body(mesh),
        mesh=mesh,
        in_specs=placed,
        out_specs=(
            P(("groups", "dp"), "space", None),
            P(("groups", "dp"), "space", None),
            P(("groups", "dp"), "space", None),
            P(("groups", "space", "dp"), "chan"),
            P(("groups", "space", "dp"), "chan"),
            P(("groups", "chan"), ("space", "dp")),
            P(("groups", "space", "dp"), "chan"),
            P(("groups", "space", "dp"), "chan"),
            P(("groups", "chan"), ("space", "dp")),
        ),
        check_vma=False,
    )
```

```python
import functools

import jax
import jax.numpy as jnp
from jax import lax
from jax.experimental import pallas as pl
from jax.experimental.pallas import tpu as pltpu
from jax.sharding import PartitionSpec as P

CAP = 16


def times_transposed(left, right):
    return lax.dot_general(
        left, right, (((1,), (1,)), ((), ())), preferred_element_type=jnp.float32
    )


def left_transposed(left, right):
    return lax.dot_general(
        left, right, (((0,), (0,)), ((), ())), preferred_element_type=jnp.float32
    )


def exact_product(left, right):
    return jnp.dot(left, right, preferred_element_type=jnp.float32, precision=lax.Precision.HIGHEST)


def region_plan(sender, live_count, node_total, regions, own_region, slot_total):
    owners = sender // node_total
    local_row = sender - owners * node_total
    remote = owners != own_region
    edge_total = sender.shape[0]
    live_mask = (jnp.arange(edge_total) < live_count[0]).astype(jnp.float32)
    by_owner = ((owners[:, None] == jnp.arange(regions)[None, :]) & remote[:, None]).astype(
        jnp.int32
    )
    earlier = jnp.cumsum(by_owner, axis=0) - by_owner
    position = jnp.sum(earlier * by_owner, axis=1)
    slot_code = jnp.where(remote, owners * slot_total + position, regions * slot_total)
    requests = (
        jnp.zeros((regions * slot_total,), jnp.int32).at[slot_code].set(local_row + 1, mode="drop")
    )
    lookup = jnp.where(remote, node_total + slot_code, local_row)
    local_scatter = (
        (local_row[None, :] == jnp.arange(node_total)[:, None]) & jnp.logical_not(remote)[None, :]
    ).astype(jnp.float32)
    return (live_mask, slot_code, requests.reshape(regions, slot_total), lookup, local_scatter)


def receiver_scatter(receiver, own_region, node_total):
    local_row = receiver - own_region * node_total
    return (local_row, (local_row[None, :] == jnp.arange(node_total)[:, None]).astype(jnp.float32))


def fetch_rows(block, wanted):
    picked = jnp.take(block, jnp.maximum(wanted - 1, 0), axis=0)
    arrived = lax.all_to_all(picked, "space", split_axis=0, concat_axis=0, tiled=True)
    return jnp.concatenate([block, arrived.reshape(-1, block.shape[1])], axis=0)


def core_total(terms):
    return lax.psum(terms, "chan")


def edge_forward(sender_rows, receiver_rows, w_send, w_recv, w_out, live_mask):
    preact = jnp.dot(sender_rows, w_send, preferred_element_type=jnp.float32) + jnp.dot(
        receiver_rows, w_recv, preferred_element_type=jnp.float32
    )
    gate_value = jax.nn.sigmoid(preact)
    activation = (preact * gate_value).astype(jnp.bfloat16)
    message = jnp.dot(activation, w_out, preferred_element_type=jnp.float32) * live_mask[:, None]
    return (preact, gate_value, activation, message)


def edge_backward(message_grad, preact, gate_value, w_out):
    hidden_grad = times_transposed(message_grad, w_out)
    return (hidden_grad * gate_value * (1.0 + preact * (1.0 - gate_value))).astype(jnp.bfloat16)


def sender_terms(preact_grad, w_send, slot_code, wanted, local_scatter, regions, slot_total):
    input_grad = times_transposed(preact_grad, w_send)
    local_part = exact_product(local_scatter, input_grad)
    outgoing = (
        jnp.zeros((regions * slot_total, input_grad.shape[1]), jnp.float32)
        .at[slot_code]
        .set(input_grad, mode="drop")
    )
    incoming = (
        lax.all_to_all(
            outgoing.reshape(regions, slot_total, -1).astype(jnp.bfloat16),
            "space",
            split_axis=0,
            concat_axis=0,
            tiled=True,
        )
        .astype(jnp.float32)
        .reshape(regions * slot_total, -1)
    )
    node_total = local_scatter.shape[0]
    owner_scatter = (wanted.reshape(-1)[None, :] - 1 == jnp.arange(node_total)[:, None]).astype(
        jnp.float32
    )
    return local_part + exact_product(owner_scatter, incoming)


def body(
    grid,
    mesh_nodes,
    cot,
    enc_send,
    enc_recv,
    enc_out,
    proc_send,
    proc_recv,
    proc_out,
    enc_sender,
    enc_receiver,
    enc_count,
    proc_sender,
    proc_receiver,
    proc_count,
):
    regions = lax.axis_size("space")
    own_region = lax.axis_index("space")
    grid_block = grid[0]
    mesh_block = mesh_nodes[0]
    cot_block = cot[0]
    grid_total = grid_block.shape[0]
    mesh_total = mesh_block.shape[0]
    enc_plan = region_plan(enc_sender, enc_count, grid_total, regions, own_region, CAP)
    proc_plan = region_plan(proc_sender, proc_count, mesh_total, regions, own_region, CAP)
    enc_wanted, proc_wanted = (
        lax.all_to_all(enc_plan[2], "space", split_axis=0, concat_axis=0, tiled=True),
        lax.all_to_all(proc_plan[2], "space", split_axis=0, concat_axis=0, tiled=True),
    )
    enc_local_recv, enc_onehot = receiver_scatter(enc_receiver, own_region, mesh_total)
    proc_local_recv, proc_onehot = receiver_scatter(proc_receiver, own_region, mesh_total)
    enc_table = fetch_rows(grid_block, enc_wanted)
    enc_senders = jnp.take(enc_table, enc_plan[3], axis=0)
    enc_receivers = jnp.take(mesh_block, enc_local_recv, axis=0)
    enc_pre, enc_gate, enc_act, enc_msg = edge_forward(
        enc_senders, enc_receivers, enc_send, enc_recv, enc_out, enc_plan[0]
    )
    enc_summed = core_total(exact_product(enc_onehot, enc_msg))
    mesh_mid = (mesh_block.astype(jnp.float32) + enc_summed).astype(jnp.bfloat16)
    proc_table = fetch_rows(mesh_mid, proc_wanted)
    proc_senders = jnp.take(proc_table, proc_plan[3], axis=0)
    proc_receivers = jnp.take(mesh_mid, proc_local_recv, axis=0)
    proc_pre, proc_gate, proc_act, proc_msg = edge_forward(
        proc_senders, proc_receivers, proc_send, proc_recv, proc_out, proc_plan[0]
    )
    proc_summed = core_total(exact_product(proc_onehot, proc_msg))
    mesh_out = (mesh_mid.astype(jnp.float32) + proc_summed).astype(jnp.bfloat16)
    proc_dmsg = jnp.where(
        proc_plan[0][:, None] > 0,
        jnp.take(cot_block, proc_local_recv, axis=0),
        jnp.zeros((), jnp.bfloat16),
    )
    proc_dpre = edge_backward(proc_dmsg, proc_pre, proc_gate, proc_out)
    proc_out_grad = left_transposed(proc_act, proc_dmsg)
    proc_send_grad = left_transposed(proc_senders, proc_dpre)
    proc_recv_grad = left_transposed(proc_receivers, proc_dpre)
    mesh_part = exact_product(proc_onehot, times_transposed(proc_dpre, proc_recv)) + sender_terms(
        proc_dpre, proc_send, proc_plan[1], proc_wanted, proc_plan[4], regions, CAP
    )
    mesh_mid_grad = cot_block.astype(jnp.float32) + core_total(mesh_part)
    enc_dmsg = jnp.where(
        enc_plan[0][:, None] > 0,
        jnp.take(mesh_mid_grad.astype(jnp.bfloat16), enc_local_recv, axis=0),
        jnp.zeros((), jnp.bfloat16),
    )
    enc_dpre = edge_backward(enc_dmsg, enc_pre, enc_gate, enc_out)
    enc_out_grad = left_transposed(enc_act, enc_dmsg)
    enc_send_grad = left_transposed(enc_senders, enc_dpre)
    enc_recv_grad = left_transposed(enc_receivers, enc_dpre)
    grid_part = sender_terms(enc_dpre, enc_send, enc_plan[1], enc_wanted, enc_plan[4], regions, CAP)
    receiver_part = exact_product(enc_onehot, times_transposed(enc_dpre, enc_recv))
    grid_summed, receiver_summed = core_total((grid_part, receiver_part))
    mesh_grad = mesh_mid_grad + receiver_summed
    shared = (
        lax.psum_scatter(enc_send_grad, ("space", "dp"), scatter_dimension=0, tiled=True),
        lax.psum_scatter(enc_recv_grad, ("space", "dp"), scatter_dimension=0, tiled=True),
        lax.psum_scatter(enc_out_grad, ("space", "dp"), scatter_dimension=1, tiled=True),
        lax.psum_scatter(proc_send_grad, ("space", "dp"), scatter_dimension=0, tiled=True),
        lax.psum_scatter(proc_recv_grad, ("space", "dp"), scatter_dimension=0, tiled=True),
        lax.psum_scatter(proc_out_grad, ("space", "dp"), scatter_dimension=1, tiled=True),
    )
    return (
        mesh_out[None],
        grid_summed[None],
        mesh_grad[None],
        shared[0],
        shared[1],
        shared[2],
        shared[3],
        shared[4],
        shared[5],
    )


F32 = jnp.float32
BF16 = jnp.bfloat16


def dot(left, right):
    return jnp.dot(left, right, preferred_element_type=F32)


def halves(values):
    high = values.astype(BF16)
    return high, (values - high.astype(F32)).astype(BF16)


def dot_split(left, values):
    high, low = halves(values)
    return dot(left, high) + dot(left, low)


def split_dot_transposed(values, right):
    high, low = halves(values)
    return times_transposed(high, right) + times_transposed(low, right)


def split_dot(values, right):
    high, low = halves(values)
    return dot(high, right) + dot(low, right)


def onehot(condition):
    return jnp.where(condition, 1.0, 0.0).astype(BF16)


def iota(shape, dim):
    return lax.broadcasted_iota(jnp.int32, shape, dim).astype(F32)


def fused_kernel(
    regions,
    samples,
    cores,
    *refs,
):
    given, refs = refs[:15], refs[15:]
    results, refs = refs[:9], refs[9:]
    held, refs = refs[:15], refs[15:]
    (
        grid_ref,
        mesh_ref,
        cot_ref,
        enc_send,
        enc_recv,
        enc_out,
        proc_send,
        proc_recv,
        proc_out,
        enc_sender,
        enc_receiver,
        enc_count,
        proc_sender,
        proc_receiver,
        proc_count,
    ) = held
    (
        mesh_out,
        grid_grad,
        mesh_grad,
        g_enc_send,
        g_enc_recv,
        g_enc_out,
        g_proc_send,
        g_proc_recv,
        g_proc_out,
    ) = results
    (
        req_out,
        req_in,
        row_out,
        row_in,
        term_out,
        term_in,
        part_out,
        part_in,
        last_out,
        last_in,
        full_grad,
        pair_out,
        pair_in,
        ring_own,
        ring_out,
        ring_in,
        send_sem,
        recv_sem,
        load_sem,
    ) = refs
    own = lax.axis_index("space")
    sample = lax.axis_index("dp")
    core = lax.axis_index("chan")
    edges = enc_sender.shape[1]
    grid_total = grid_ref.shape[0]
    mesh_total = mesh_ref.shape[0]
    slots = regions * CAP
    used = [0]

    def space_at(step):
        return lax.rem(own + step, regions)

    def core_at(step):
        return lax.rem(core + step, cores)

    def place(s, d, c):
        return {"space": s, "dp": d, "chan": c}

    def send(src, dst, target):
        index = used[0]
        used[0] += 1
        copy = pltpu.make_async_remote_copy(
            src_ref=src,
            dst_ref=dst,
            send_sem=send_sem.at[index],
            recv_sem=recv_sem.at[index],
            device_id=target,
            device_id_type=pl.DeviceIdType.MESH,
        )
        copy.start()
        return copy

    def arrive(copies):
        for copy in copies:
            copy.wait_recv()

    everything = []
    friends = []
    for c_step in range(cores):
        for s_step in range(regions):
            if c_step or s_step:
                friends.append(place(space_at(s_step), sample, core_at(c_step)))
    for d_step in range(1, samples):
        friends.append(place(own, lax.rem(sample + d_step, samples), core))
    loads = [
        pltpu.make_async_copy(given[i], held[i], load_sem.at[i]) for i in range(len(given))
    ]
    for i in (9, 10, 11, 12, 13, 14, 0, 3, 1, 4, 2, 8, 5, 6, 7):
        loads[i].start()
    barrier = pltpu.get_barrier_semaphore()
    for friend in friends:
        pl.semaphore_signal(
            barrier, inc=1, device_id=friend, device_id_type=pl.DeviceIdType.MESH
        )

    for i in range(9, 15):
        loads[i].wait()
    owner_rows = 16
    before = onehot(iota((edges, edges), 0) < iota((edges, edges), 1))
    owner_id = iota((owner_rows, edges), 0)
    own_id = own.astype(F32)

    def rows_of(sender_ref, receiver_ref, count_ref, total):
        sender = sender_ref[...].astype(F32)
        low = owner_id * total
        owned = (sender >= low) & (sender < low + total)
        local = (sender >= own_id * total) & (sender < own_id * total + total)
        by_owner = jnp.where(owned & (owner_id != own_id), 1.0, 0.0)
        earlier = dot(by_owner.astype(BF16), before)
        code = jnp.sum(by_owner * (owner_id * CAP + earlier), axis=0, keepdims=True)
        owner = jnp.sum(by_owner * owner_id, axis=0, keepdims=True)
        code = jnp.where(local, -1.0, code)
        local_row = jnp.where(local, sender - own_id * total, -1.0)
        wanted = sender - owner * total + 1.0
        receiver = receiver_ref[...].astype(F32) - own_id * mesh_total
        alive = iota((1, edges), 1) < count_ref[...].astype(F32)
        live_receiver = jnp.where(alive, receiver, -1.0)
        match = code == iota((slots, edges), 0)
        request = jnp.sum(jnp.where(match, wanted, 0.0), axis=1, keepdims=True)
        return (local_row, code, receiver, live_receiver), onehot(match), request

    enc_rows, enc_match, enc_request = rows_of(enc_sender, enc_receiver, enc_count, grid_total)
    proc_rows, proc_match, proc_request = rows_of(
        proc_sender, proc_receiver, proc_count, mesh_total
    )
    req_out[:, 0:CAP, :] = jnp.broadcast_to(enc_request, (slots, 128)).reshape(regions, CAP, 128)
    req_out[:, CAP : 2 * CAP, :] = jnp.broadcast_to(proc_request, (slots, 128)).reshape(
        regions, CAP, 128
    )
    req_in[own] = jnp.zeros(req_in.shape[1:], F32)
    for graph in range(2):
        row_in[graph, own] = jnp.zeros(row_in.shape[2:], BF16)
        for c_step in range(cores):
            term_in[graph, c_step, own] = jnp.zeros(term_in.shape[3:], BF16)

    pl.semaphore_wait(barrier, len(friends))
    requests = [
        send(req_out.at[space_at(step)], req_in.at[own], place(space_at(step), sample, core))
        for step in range(1, regions)
    ]
    everything += requests

    columns = jnp.transpose(jnp.concatenate(list(enc_rows) + list(proc_rows), axis=0))

    def tables(rows, first, total):
        by_edge = [columns[:, first + i : first + i + 1] for i in range(4)]
        return (
            onehot(by_edge[0] == iota((edges, total), 1)),
            onehot(by_edge[1] == iota((edges, slots), 1)),
            onehot(by_edge[2] == iota((edges, mesh_total), 1)),
            onehot(by_edge[3] == iota((edges, mesh_total), 1)),
            onehot(rows[0] == iota((total, edges), 0)),
            onehot(rows[2] == iota((mesh_total, edges), 0)),
            onehot(rows[3] == iota((mesh_total, edges), 0)),
        )

    e_pick, e_far, e_recv, e_live, e_pick_t, e_recv_t, e_live_t = tables(
        enc_rows, 0, grid_total
    )
    p_pick, p_far, p_recv, p_live, p_pick_t, p_recv_t, p_live_t = tables(
        proc_rows, 4, mesh_total
    )
    for i in range(9):
        loads[i].wait()
    grid_block = grid_ref[...]
    mesh_block = mesh_ref[...]
    cot_block = cot_ref[...]
    enc_pre = dot_split(e_pick, dot(grid_block, enc_send[...])) + dot_split(
        e_recv, dot(mesh_block, enc_recv[...])
    )
    proc_hidden = dot_split(p_live, times_transposed(cot_block, proc_out[...]))

    def picks(graph, total):
        asked = req_in[:, graph * CAP : (graph + 1) * CAP, :].reshape(slots, 128)
        return onehot(asked[:, 0:1] == iota((slots, total), 1) + 1.0)

    def send_rows(graph, pick, block):
        row_out[graph] = dot(pick, block).astype(BF16).reshape(regions, CAP, -1)
        return [
            send(
                row_out.at[graph, space_at(step)],
                row_in.at[graph, own],
                place(space_at(step), sample, core),
            )
            for step in range(1, regions)
        ]

    def far_rows(graph):
        return row_in[graph].reshape(slots, -1)

    arrive(requests)
    enc_asked = picks(0, grid_total)
    rows_sent = send_rows(0, enc_asked, grid_block)
    everything += rows_sent
    proc_asked = picks(1, mesh_total)
    arrive(rows_sent)

    enc_pre = enc_pre + dot_split(e_far, dot(far_rows(0), enc_send[...]))
    enc_gate = jax.nn.sigmoid(enc_pre)
    enc_act_sum = dot(e_live_t, (enc_pre * enc_gate).astype(BF16))
    enc_sum = split_dot(enc_act_sum, enc_out[...])
    other = place(own, sample, core_at(1))
    part_out[0] = enc_sum
    swapped = send(part_out.at[0], part_in.at[0], other)
    everything.append(swapped)
    enc_slope = enc_gate * (1.0 + enc_pre * (1.0 - enc_gate))
    swapped.wait_recv()
    mesh_mid = (mesh_block.astype(F32) + (part_out[0] + part_in[0])).astype(BF16)

    rows_sent = send_rows(1, proc_asked, mesh_mid)
    everything += rows_sent
    proc_pre = dot_split(p_pick, dot(mesh_mid, proc_send[...])) + dot_split(
        p_recv, dot(mesh_mid, proc_recv[...])
    )
    arrive(rows_sent)
    proc_pre = proc_pre + dot_split(p_far, dot(far_rows(1), proc_send[...]))
    proc_gate = jax.nn.sigmoid(proc_pre)
    proc_dpre = (proc_hidden * (proc_gate * (1.0 + proc_pre * (1.0 - proc_gate)))).astype(BF16)

    def send_terms(graph, far, weights):
        term_out[graph] = times_transposed(far, weights).astype(BF16).reshape(regions, CAP, -1)
        copies = []
        for step in range(1, regions):
            for c_step in range(cores):
                copies.append(
                    send(
                        term_out.at[graph, space_at(step)],
                        term_in.at[graph, core, own],
                        place(space_at(step), sample, core_at(c_step)),
                    )
                )
        return copies

    def returned(graph, asked):
        return left_transposed(
            jnp.concatenate([asked] * cores, axis=0),
            term_in[graph].reshape(cores * slots, -1),
        )

    proc_far = dot(proc_match, proc_dpre).astype(BF16)
    terms = send_terms(1, proc_far, proc_send[...])
    everything += terms
    proc_by_sender = dot(p_pick_t, proc_dpre)
    proc_by_receiver = dot(p_recv_t, proc_dpre)
    part_out[1] = split_dot_transposed(proc_by_receiver, proc_recv[...]) + split_dot_transposed(
        proc_by_sender, proc_send[...]
    )
    swapped = send(part_out.at[1], part_in.at[1], other)
    everything.append(swapped)

    shard = full_grad.shape[3]

    def share(index, gradient):
        for s in range(regions):
            for d in range(samples):
                piece = gradient[(s * samples + d) * shard : (s * samples + d + 1) * shard]
                full_grad[index, d, s] = piece
                pair_out[index, d, s] = piece.astype(BF16)
        copies = []
        for step in range(1, samples):
            target = lax.rem(sample + step, samples)
            copies.append(
                send(
                    pair_out.at[index, target],
                    pair_in.at[index, step - 1],
                    place(own, target, core),
                )
            )
        return copies

    def pass_on(index, copies):
        arrive(copies)
        total = full_grad[index, sample]
        for step in range(1, samples):
            total = total + pair_in[index, step - 1].astype(F32)
        ring_own[index] = total
        ring_out[index] = total.astype(BF16)
        return [
            send(
                ring_out.at[index, space_at(step)],
                ring_in.at[index, step - 1],
                place(space_at(step), sample, core),
            )
            for step in range(1, regions)
        ]

    def finish(index, copies):
        arrive(copies)
        total = ring_own[index, own]
        for step in range(1, regions):
            total = total + ring_in[index, step - 1].astype(F32)
        return total

    proc_act_sum = dot(p_live_t, (proc_pre * proc_gate).astype(BF16))
    shared = {}
    shared[5] = share(5, left_transposed(cot_block, proc_act_sum.astype(BF16)))
    shared[3] = share(
        3,
        left_transposed(mesh_mid, proc_by_sender.astype(BF16))
        + left_transposed(far_rows(1), proc_far),
    )
    shared[4] = share(4, left_transposed(mesh_mid, proc_by_receiver.astype(BF16)))
    part_out[2] = split_dot(proc_act_sum, proc_out[...])
    out_swap = send(part_out.at[2], part_in.at[2], other)
    everything.append(out_swap)
    passed = {}

    arrive(terms)
    swapped.wait_recv()
    mesh_mid_grad = cot_block.astype(F32) + (
        (part_out[1] + part_in[1]) + returned(1, proc_asked)
    )

    mid_rounded = mesh_mid_grad.astype(BF16)
    passed[5] = pass_on(5, shared[5])
    enc_hidden = dot_split(e_live, times_transposed(mid_rounded, enc_out[...]))
    enc_dpre = (enc_hidden * enc_slope).astype(BF16)
    shared[2] = share(2, left_transposed(mid_rounded, enc_act_sum.astype(BF16)))
    enc_by_sender = dot(e_pick_t, enc_dpre)
    enc_by_receiver = dot(e_recv_t, enc_dpre)
    enc_far = dot(enc_match, enc_dpre).astype(BF16)
    passed[3] = pass_on(3, shared[3])
    shared[0] = share(
        0,
        left_transposed(grid_block, enc_by_sender.astype(BF16))
        + left_transposed(far_rows(0), enc_far),
    )
    shared[1] = share(1, left_transposed(mesh_block, enc_by_receiver.astype(BF16)))
    passed[4] = pass_on(4, shared[4])
    terms = send_terms(0, enc_far, enc_send[...])
    everything += terms
    last_out[0:grid_total] = split_dot_transposed(enc_by_sender, enc_send[...])
    last_out[grid_total : grid_total + mesh_total] = split_dot_transposed(
        enc_by_receiver, enc_recv[...]
    )
    last_swap = send(last_out, last_in, other)
    everything.append(last_swap)

    for index in (2, 0, 1):
        passed[index] = pass_on(index, shared[index])
    for index in shared:
        everything += shared[index] + passed[index]

    out_swap.wait_recv()
    mesh_out[...] = (mesh_mid.astype(F32) + (part_out[2] + part_in[2])).astype(BF16)
    arrive(terms)
    last_swap.wait_recv()
    grid_grad[...] = (last_out[0:grid_total] + last_in[0:grid_total]) + returned(0, enc_asked)
    tail = slice(grid_total, grid_total + mesh_total)
    mesh_grad[...] = mesh_mid_grad + (last_out[tail] + last_in[tail])

    g_proc_out[...] = finish(5, passed[5])
    g_proc_send[...] = finish(3, passed[3])
    g_proc_recv[...] = finish(4, passed[4])
    g_enc_out[...] = finish(2, passed[2])
    g_enc_send[...] = finish(0, passed[0])
    g_enc_recv[...] = finish(1, passed[1])
    for copy in everything:
        copy.wait_send()


def place_kernel(*refs):
    sources, targets, sems = refs[:9], refs[9:18], refs[18]
    copies = [
        pltpu.make_async_copy(sources[i], targets[i], sems.at[i]) for i in range(9)
    ]
    for copy in copies:
        copy.start()
    for copy in copies:
        copy.wait()


def fused_body(regions, samples, cores, grid, mesh_nodes, cot, *rest):
    weights = rest[:6]
    given = [grid[0], mesh_nodes[0], cot[0], *weights]
    given += [index.reshape(1, -1) for index in rest[6:]]
    grid_total, width = grid.shape[1:]
    mesh_total = mesh_nodes.shape[1]
    hidden = weights[0].shape[1]
    shard = width // (regions * samples)
    last_total = grid_total + mesh_total
    copies = (regions - 1) * (3 + 2 * cores + 6) + 6 * (samples - 1) + 4
    vmem = pl.BlockSpec(memory_space=pltpu.VMEM)
    outs = pl.pallas_call(
        functools.partial(fused_kernel, regions, samples, cores),
        out_shape=(
            jax.ShapeDtypeStruct((mesh_total, width), BF16),
            jax.ShapeDtypeStruct((grid_total, width), F32),
            jax.ShapeDtypeStruct((mesh_total, width), F32),
            jax.ShapeDtypeStruct((shard, hidden), F32),
            jax.ShapeDtypeStruct((shard, hidden), F32),
            jax.ShapeDtypeStruct((shard, hidden), F32),
            jax.ShapeDtypeStruct((shard, hidden), F32),
            jax.ShapeDtypeStruct((shard, hidden), F32),
            jax.ShapeDtypeStruct((shard, hidden), F32),
        ),
        in_specs=[pl.BlockSpec(memory_space=pl.ANY)] * 15,
        out_specs=(vmem,) * 9,
        scratch_shapes=[pltpu.VMEM(array.shape, array.dtype) for array in given]
        + [
            pltpu.VMEM((regions, 2 * CAP, 128), F32),
            pltpu.VMEM((regions, 2 * CAP, 128), F32),
            pltpu.VMEM((2, regions, CAP, width), BF16),
            pltpu.VMEM((2, regions, CAP, width), BF16),
            pltpu.VMEM((2, regions, CAP, width), BF16),
            pltpu.VMEM((2, cores, regions, CAP, width), BF16),
            pltpu.VMEM((3, mesh_total, width), F32),
            pltpu.VMEM((3, mesh_total, width), F32),
            pltpu.VMEM((last_total, width), F32),
            pltpu.VMEM((last_total, width), F32),
            pltpu.VMEM((6, samples, regions, shard, hidden), F32),
            pltpu.VMEM((6, samples, regions, shard, hidden), BF16),
            pltpu.VMEM((6, samples - 1, regions, shard, hidden), BF16),
            pltpu.VMEM((6, regions, shard, hidden), F32),
            pltpu.VMEM((6, regions, shard, hidden), BF16),
            pltpu.VMEM((6, regions - 1, shard, hidden), BF16),
            pltpu.SemaphoreType.DMA((copies,)),
            pltpu.SemaphoreType.DMA((copies,)),
            pltpu.SemaphoreType.DMA((15,)),
        ],
        compiler_params=pltpu.CompilerParams(
            collective_id=0, has_side_effects=True, vmem_limit_bytes=58 * 2**20
        ),
    )(*given)
    outs = pl.pallas_call(
        place_kernel,
        out_shape=[jax.ShapeDtypeStruct(out.shape, out.dtype) for out in outs],
        in_specs=[vmem] * 9,
        out_specs=[pl.BlockSpec(memory_space=pl.ANY)] * 9,
        scratch_shapes=[pltpu.SemaphoreType.DMA((9,))],
    )(*outs)
    gradients = [out.T if i in (2, 5) else out for i, out in enumerate(outs[3:])]
    return (outs[0][None], outs[1][None], outs[2][None], *gradients)


def chosen_body(mesh):
    regions, samples, cores = (mesh.shape[name] for name in ("space", "dp", "chan"))
    shards = regions * samples

    def run(*args):
        width = args[0].shape[2]
        if regions > 16 or samples < 2 or cores != 2 or width % (16 * shards):
            return body(*args)
        return fused_body(regions, samples, cores, *args)

    return run


def solution(mesh):
    placed = (
        P(("groups", "dp"), "space", None),
        P(("groups", "dp"), "space", None),
        P(("groups", "dp"), "space", None),
        P(None, "chan"),
        P(None, "chan"),
        P("chan", None),
        P(None, "chan"),
        P(None, "chan"),
        P("chan", None),
        P("space"),
        P("space"),
        P("space"),
        P("space"),
        P("space"),
        P("space"),
    )
    return jax.shard_map(
        chosen_body(mesh),
        mesh=mesh,
        in_specs=placed,
        out_specs=(
            P(("groups", "dp"), "space", None),
            P(("groups", "dp"), "space", None),
            P(("groups", "dp"), "space", None),
            P(("groups", "space", "dp"), "chan"),
            P(("groups", "space", "dp"), "chan"),
            P(("groups", "chan"), ("space", "dp")),
            P(("groups", "space", "dp"), "chan"),
            P(("groups", "space", "dp"), "chan"),
            P(("groups", "chan"), ("space", "dp")),
        ),
        check_vma=False,
    )
```

```python
import functools

import jax
import jax.numpy as jnp
from jax import lax
from jax.experimental import pallas as pl
from jax.experimental.pallas import tpu as pltpu
from jax.sharding import PartitionSpec as P

CAP = 16


def times_transposed(left, right):
    return lax.dot_general(
        left, right, (((1,), (1,)), ((), ())), preferred_element_type=jnp.float32
    )


def left_transposed(left, right):
    return lax.dot_general(
        left, right, (((0,), (0,)), ((), ())), preferred_element_type=jnp.float32
    )


def exact_product(left, right):
    return jnp.dot(left, right, preferred_element_type=jnp.float32, precision=lax.Precision.HIGHEST)


def region_plan(sender, live_count, node_total, regions, own_region, slot_total):
    owners = sender // node_total
    local_row = sender - owners * node_total
    remote = owners != own_region
    edge_total = sender.shape[0]
    live_mask = (jnp.arange(edge_total) < live_count[0]).astype(jnp.float32)
    by_owner = ((owners[:, None] == jnp.arange(regions)[None, :]) & remote[:, None]).astype(
        jnp.int32
    )
    earlier = jnp.cumsum(by_owner, axis=0) - by_owner
    position = jnp.sum(earlier * by_owner, axis=1)
    slot_code = jnp.where(remote, owners * slot_total + position, regions * slot_total)
    requests = (
        jnp.zeros((regions * slot_total,), jnp.int32).at[slot_code].set(local_row + 1, mode="drop")
    )
    lookup = jnp.where(remote, node_total + slot_code, local_row)
    local_scatter = (
        (local_row[None, :] == jnp.arange(node_total)[:, None]) & jnp.logical_not(remote)[None, :]
    ).astype(jnp.float32)
    return (live_mask, slot_code, requests.reshape(regions, slot_total), lookup, local_scatter)


def receiver_scatter(receiver, own_region, node_total):
    local_row = receiver - own_region * node_total
    return (local_row, (local_row[None, :] == jnp.arange(node_total)[:, None]).astype(jnp.float32))


def fetch_rows(block, wanted):
    picked = jnp.take(block, jnp.maximum(wanted - 1, 0), axis=0)
    arrived = lax.all_to_all(picked, "space", split_axis=0, concat_axis=0, tiled=True)
    return jnp.concatenate([block, arrived.reshape(-1, block.shape[1])], axis=0)


def core_total(terms):
    return lax.psum(terms, "chan")


def edge_forward(sender_rows, receiver_rows, w_send, w_recv, w_out, live_mask):
    preact = jnp.dot(sender_rows, w_send, preferred_element_type=jnp.float32) + jnp.dot(
        receiver_rows, w_recv, preferred_element_type=jnp.float32
    )
    gate_value = jax.nn.sigmoid(preact)
    activation = (preact * gate_value).astype(jnp.bfloat16)
    message = jnp.dot(activation, w_out, preferred_element_type=jnp.float32) * live_mask[:, None]
    return (preact, gate_value, activation, message)


def edge_backward(message_grad, preact, gate_value, w_out):
    hidden_grad = times_transposed(message_grad, w_out)
    return (hidden_grad * gate_value * (1.0 + preact * (1.0 - gate_value))).astype(jnp.bfloat16)


def sender_terms(preact_grad, w_send, slot_code, wanted, local_scatter, regions, slot_total):
    input_grad = times_transposed(preact_grad, w_send)
    local_part = exact_product(local_scatter, input_grad)
    outgoing = (
        jnp.zeros((regions * slot_total, input_grad.shape[1]), jnp.float32)
        .at[slot_code]
        .set(input_grad, mode="drop")
    )
    incoming = (
        lax.all_to_all(
            outgoing.reshape(regions, slot_total, -1).astype(jnp.bfloat16),
            "space",
            split_axis=0,
            concat_axis=0,
            tiled=True,
        )
        .astype(jnp.float32)
        .reshape(regions * slot_total, -1)
    )
    node_total = local_scatter.shape[0]
    owner_scatter = (wanted.reshape(-1)[None, :] - 1 == jnp.arange(node_total)[:, None]).astype(
        jnp.float32
    )
    return local_part + exact_product(owner_scatter, incoming)


def body(
    grid,
    mesh_nodes,
    cot,
    enc_send,
    enc_recv,
    enc_out,
    proc_send,
    proc_recv,
    proc_out,
    enc_sender,
    enc_receiver,
    enc_count,
    proc_sender,
    proc_receiver,
    proc_count,
):
    regions = lax.axis_size("space")
    own_region = lax.axis_index("space")
    grid_block = grid[0]
    mesh_block = mesh_nodes[0]
    cot_block = cot[0]
    grid_total = grid_block.shape[0]
    mesh_total = mesh_block.shape[0]
    enc_plan = region_plan(enc_sender, enc_count, grid_total, regions, own_region, CAP)
    proc_plan = region_plan(proc_sender, proc_count, mesh_total, regions, own_region, CAP)
    enc_wanted, proc_wanted = (
        lax.all_to_all(enc_plan[2], "space", split_axis=0, concat_axis=0, tiled=True),
        lax.all_to_all(proc_plan[2], "space", split_axis=0, concat_axis=0, tiled=True),
    )
    enc_local_recv, enc_onehot = receiver_scatter(enc_receiver, own_region, mesh_total)
    proc_local_recv, proc_onehot = receiver_scatter(proc_receiver, own_region, mesh_total)
    enc_table = fetch_rows(grid_block, enc_wanted)
    enc_senders = jnp.take(enc_table, enc_plan[3], axis=0)
    enc_receivers = jnp.take(mesh_block, enc_local_recv, axis=0)
    enc_pre, enc_gate, enc_act, enc_msg = edge_forward(
        enc_senders, enc_receivers, enc_send, enc_recv, enc_out, enc_plan[0]
    )
    enc_summed = core_total(exact_product(enc_onehot, enc_msg))
    mesh_mid = (mesh_block.astype(jnp.float32) + enc_summed).astype(jnp.bfloat16)
    proc_table = fetch_rows(mesh_mid, proc_wanted)
    proc_senders = jnp.take(proc_table, proc_plan[3], axis=0)
    proc_receivers = jnp.take(mesh_mid, proc_local_recv, axis=0)
    proc_pre, proc_gate, proc_act, proc_msg = edge_forward(
        proc_senders, proc_receivers, proc_send, proc_recv, proc_out, proc_plan[0]
    )
    proc_summed = core_total(exact_product(proc_onehot, proc_msg))
    mesh_out = (mesh_mid.astype(jnp.float32) + proc_summed).astype(jnp.bfloat16)
    proc_dmsg = jnp.where(
        proc_plan[0][:, None] > 0,
        jnp.take(cot_block, proc_local_recv, axis=0),
        jnp.zeros((), jnp.bfloat16),
    )
    proc_dpre = edge_backward(proc_dmsg, proc_pre, proc_gate, proc_out)
    proc_out_grad = left_transposed(proc_act, proc_dmsg)
    proc_send_grad = left_transposed(proc_senders, proc_dpre)
    proc_recv_grad = left_transposed(proc_receivers, proc_dpre)
    mesh_part = exact_product(proc_onehot, times_transposed(proc_dpre, proc_recv)) + sender_terms(
        proc_dpre, proc_send, proc_plan[1], proc_wanted, proc_plan[4], regions, CAP
    )
    mesh_mid_grad = cot_block.astype(jnp.float32) + core_total(mesh_part)
    enc_dmsg = jnp.where(
        enc_plan[0][:, None] > 0,
        jnp.take(mesh_mid_grad.astype(jnp.bfloat16), enc_local_recv, axis=0),
        jnp.zeros((), jnp.bfloat16),
    )
    enc_dpre = edge_backward(enc_dmsg, enc_pre, enc_gate, enc_out)
    enc_out_grad = left_transposed(enc_act, enc_dmsg)
    enc_send_grad = left_transposed(enc_senders, enc_dpre)
    enc_recv_grad = left_transposed(enc_receivers, enc_dpre)
    grid_part = sender_terms(enc_dpre, enc_send, enc_plan[1], enc_wanted, enc_plan[4], regions, CAP)
    receiver_part = exact_product(enc_onehot, times_transposed(enc_dpre, enc_recv))
    grid_summed, receiver_summed = core_total((grid_part, receiver_part))
    mesh_grad = mesh_mid_grad + receiver_summed
    shared = (
        lax.psum_scatter(enc_send_grad, ("space", "dp"), scatter_dimension=0, tiled=True),
        lax.psum_scatter(enc_recv_grad, ("space", "dp"), scatter_dimension=0, tiled=True),
        lax.psum_scatter(enc_out_grad, ("space", "dp"), scatter_dimension=1, tiled=True),
        lax.psum_scatter(proc_send_grad, ("space", "dp"), scatter_dimension=0, tiled=True),
        lax.psum_scatter(proc_recv_grad, ("space", "dp"), scatter_dimension=0, tiled=True),
        lax.psum_scatter(proc_out_grad, ("space", "dp"), scatter_dimension=1, tiled=True),
    )
    return (
        mesh_out[None],
        grid_summed[None],
        mesh_grad[None],
        shared[0],
        shared[1],
        shared[2],
        shared[3],
        shared[4],
        shared[5],
    )


F32 = jnp.float32
BF16 = jnp.bfloat16


def dot(left, right):
    return jnp.dot(left, right, preferred_element_type=F32)


def halves(values):
    high = values.astype(BF16)
    return high, (values - high.astype(F32)).astype(BF16)


def dot_split(left, values):
    high, low = halves(values)
    return dot(left, high) + dot(left, low)


def split_dot_transposed(values, right):
    high, low = halves(values)
    return times_transposed(high, right) + times_transposed(low, right)


def split_dot(values, right):
    high, low = halves(values)
    return dot(high, right) + dot(low, right)


def onehot(condition):
    return jnp.where(condition, 1.0, 0.0).astype(BF16)


def iota(shape, dim):
    return lax.broadcasted_iota(jnp.int32, shape, dim).astype(F32)


def fused_kernel(
    regions,
    samples,
    cores,
    *refs,
):
    given, refs = refs[:15], refs[15:]
    results, refs = refs[:9], refs[9:]
    held, refs = refs[:15], refs[15:]
    (
        grid_ref,
        mesh_ref,
        cot_ref,
        enc_send,
        enc_recv,
        enc_out,
        proc_send,
        proc_recv,
        proc_out,
        enc_sender,
        enc_receiver,
        enc_count,
        proc_sender,
        proc_receiver,
        proc_count,
    ) = held
    (
        mesh_out,
        grid_grad,
        mesh_grad,
        g_enc_send,
        g_enc_recv,
        g_enc_out,
        g_proc_send,
        g_proc_recv,
        g_proc_out,
    ) = results
    (
        req_out,
        req_in,
        row_out,
        row_in,
        term_out,
        term_in,
        part_out,
        part_in,
        last_out,
        last_in,
        full_grad,
        pair_out,
        pair_in,
        ring_own,
        ring_out,
        ring_in,
        send_sem,
        recv_sem,
        load_sem,
        mid_out,
        left_in,
        factor_out,
        factor_in,
    ) = refs
    own = lax.axis_index("space")
    sample = lax.axis_index("dp")
    core = lax.axis_index("chan")
    edges = enc_sender.shape[1]
    grid_total = grid_ref.shape[0]
    mesh_total = mesh_ref.shape[0]
    slots = regions * CAP
    used = [0]

    def space_at(step):
        return lax.rem(own + step, regions)

    def core_at(step):
        return lax.rem(core + step, cores)

    def place(s, d, c):
        return {"space": s, "dp": d, "chan": c}

    def send(src, dst, target):
        index = used[0]
        used[0] += 1
        copy = pltpu.make_async_remote_copy(
            src_ref=src,
            dst_ref=dst,
            send_sem=send_sem.at[index],
            recv_sem=recv_sem.at[index],
            device_id=target,
            device_id_type=pl.DeviceIdType.MESH,
        )
        copy.start()
        return copy

    def arrive(copies):
        for copy in copies:
            copy.wait_recv()

    everything = []
    friends = []
    for c_step in range(cores):
        for s_step in range(regions):
            if c_step or s_step:
                friends.append(place(space_at(s_step), sample, core_at(c_step)))
    for d_step in range(1, samples):
        friends.append(place(own, lax.rem(sample + d_step, samples), core))
    loads = [
        pltpu.make_async_copy(given[i], held[i], load_sem.at[i]) for i in range(len(given))
    ]
    for i in (9, 10, 11, 12, 13, 14, 0, 3, 1, 4, 2, 8, 5, 6, 7):
        loads[i].start()
    barrier = pltpu.get_barrier_semaphore()
    for friend in friends:
        pl.semaphore_signal(
            barrier, inc=1, device_id=friend, device_id_type=pl.DeviceIdType.MESH
        )

    for i in range(9, 15):
        loads[i].wait()
    owner_rows = 16
    before = onehot(iota((edges, edges), 0) < iota((edges, edges), 1))
    owner_id = iota((owner_rows, edges), 0)
    own_id = own.astype(F32)

    def rows_of(sender_ref, receiver_ref, count_ref, total):
        sender = sender_ref[...].astype(F32)
        low = owner_id * total
        owned = (sender >= low) & (sender < low + total)
        local = (sender >= own_id * total) & (sender < own_id * total + total)
        by_owner = jnp.where(owned & (owner_id != own_id), 1.0, 0.0)
        earlier = dot(by_owner.astype(BF16), before)
        code = jnp.sum(by_owner * (owner_id * CAP + earlier), axis=0, keepdims=True)
        owner = jnp.sum(by_owner * owner_id, axis=0, keepdims=True)
        code = jnp.where(local, -1.0, code)
        local_row = jnp.where(local, sender - own_id * total, -1.0)
        wanted = sender - owner * total + 1.0
        receiver = receiver_ref[...].astype(F32) - own_id * mesh_total
        alive = iota((1, edges), 1) < count_ref[...].astype(F32)
        live_receiver = jnp.where(alive, receiver, -1.0)
        match = code == iota((slots, edges), 0)
        request = jnp.sum(jnp.where(match, wanted, 0.0), axis=1, keepdims=True)
        return (local_row, code, receiver, live_receiver), onehot(match), request

    enc_rows, enc_match, enc_request = rows_of(enc_sender, enc_receiver, enc_count, grid_total)
    proc_rows, proc_match, proc_request = rows_of(
        proc_sender, proc_receiver, proc_count, mesh_total
    )
    req_out[:, 0:CAP, :] = jnp.broadcast_to(enc_request, (slots, 128)).reshape(regions, CAP, 128)
    req_out[:, CAP : 2 * CAP, :] = jnp.broadcast_to(proc_request, (slots, 128)).reshape(
        regions, CAP, 128
    )
    req_in[own] = jnp.zeros(req_in.shape[1:], F32)
    for graph in range(2):
        row_in[graph, own] = jnp.zeros(row_in.shape[2:], BF16)
        for c_step in range(cores):
            term_in[graph, c_step, own] = jnp.zeros(term_in.shape[3:], BF16)

    pl.semaphore_wait(barrier, len(friends))
    requests = [
        send(req_out.at[space_at(step)], req_in.at[own], place(space_at(step), sample, core))
        for step in range(1, regions)
    ]
    everything += requests

    columns = jnp.transpose(jnp.concatenate(list(enc_rows) + list(proc_rows), axis=0))

    def tables(rows, first, total):
        by_edge = [columns[:, first + i : first + i + 1] for i in range(4)]
        return (
            onehot(by_edge[0] == iota((edges, total), 1)),
            onehot(by_edge[1] == iota((edges, slots), 1)),
            onehot(by_edge[2] == iota((edges, mesh_total), 1)),
            onehot(by_edge[3] == iota((edges, mesh_total), 1)),
            onehot(rows[0] == iota((total, edges), 0)),
            onehot(rows[2] == iota((mesh_total, edges), 0)),
            onehot(rows[3] == iota((mesh_total, edges), 0)),
        )

    e_pick, e_far, e_recv, e_live, e_pick_t, e_recv_t, e_live_t = tables(
        enc_rows, 0, grid_total
    )
    p_pick, p_far, p_recv, p_live, p_pick_t, p_recv_t, p_live_t = tables(
        proc_rows, 4, mesh_total
    )
    for i in range(9):
        loads[i].wait()
    grid_block = grid_ref[...]
    mesh_block = mesh_ref[...]
    cot_block = cot_ref[...]

    def to_samples(src, dst):
        return [
            send(src, dst.at[step - 1], place(own, lax.rem(sample + step, samples), core))
            for step in range(1, samples)
        ]

    slot_of = {5: 0, 1: 1, 4: 2}
    left_of = {5: cot_ref, 1: mesh_ref, 4: mid_out}
    lefts = {5: to_samples(cot_ref, left_in.at[0]), 1: to_samples(mesh_ref, left_in.at[1])}
    enc_pre = dot_split(e_pick, dot(grid_block, enc_send[...])) + dot_split(
        e_recv, dot(mesh_block, enc_recv[...])
    )
    proc_hidden = dot_split(p_live, times_transposed(cot_block, proc_out[...]))

    def picks(graph, total):
        asked = req_in[:, graph * CAP : (graph + 1) * CAP, :].reshape(slots, 128)
        return onehot(asked[:, 0:1] == iota((slots, total), 1) + 1.0)

    def send_rows(graph, pick, block):
        row_out[graph] = dot(pick, block).astype(BF16).reshape(regions, CAP, -1)
        return [
            send(
                row_out.at[graph, space_at(step)],
                row_in.at[graph, own],
                place(space_at(step), sample, core),
            )
            for step in range(1, regions)
        ]

    def far_rows(graph):
        return row_in[graph].reshape(slots, -1)

    arrive(requests)
    enc_asked = picks(0, grid_total)
    rows_sent = send_rows(0, enc_asked, grid_block)
    everything += rows_sent
    proc_asked = picks(1, mesh_total)
    arrive(rows_sent)

    enc_pre = enc_pre + dot_split(e_far, dot(far_rows(0), enc_send[...]))
    enc_gate = jax.nn.sigmoid(enc_pre)
    enc_act_sum = dot(e_live_t, (enc_pre * enc_gate).astype(BF16))
    enc_sum = split_dot(enc_act_sum, enc_out[...])
    other = place(own, sample, core_at(1))
    part_out[0] = enc_sum
    swapped = send(part_out.at[0], part_in.at[0], other)
    everything.append(swapped)
    enc_slope = enc_gate * (1.0 + enc_pre * (1.0 - enc_gate))
    swapped.wait_recv()
    mesh_mid = (mesh_block.astype(F32) + (part_out[0] + part_in[0])).astype(BF16)

    shard = full_grad.shape[3]

    def share(index, gradient):
        for s in range(regions):
            for d in range(samples):
                piece = gradient[(s * samples + d) * shard : (s * samples + d + 1) * shard]
                full_grad[index, d, s] = piece
                pair_out[index, d, s] = piece.astype(BF16)
        copies = []
        for step in range(1, samples):
            target = lax.rem(sample + step, samples)
            copies.append(
                send(
                    pair_out.at[index, target],
                    pair_in.at[index, step - 1],
                    place(own, target, core),
                )
            )
        return copies

    def share_factor(index, factor):
        slot = slot_of[index]
        factor_out[slot] = factor.astype(BF16)
        return to_samples(factor_out.at[slot], factor_in.at[slot])

    def pass_on(index, copies):
        arrive(copies)
        if index in slot_of:
            slot = slot_of[index]
            arrive(lefts[index])
            gradient = left_transposed(left_of[index][...], factor_out[slot])
            for step in range(1, samples):
                gradient = gradient + left_transposed(
                    left_in[slot, step - 1], factor_in[slot, step - 1]
                )
            for s in range(regions):
                for d in range(samples):
                    first = (s * samples + d) * shard
                    full_grad[index, d, s] = gradient[first : first + shard]
            total = full_grad[index, sample]
        else:
            total = full_grad[index, sample]
            for step in range(1, samples):
                total = total + pair_in[index, step - 1].astype(F32)
        ring_own[index] = total
        ring_out[index] = total.astype(BF16)
        return [
            send(
                ring_out.at[index, space_at(step)],
                ring_in.at[index, step - 1],
                place(space_at(step), sample, core),
            )
            for step in range(1, regions)
        ]

    def finish(index, copies):
        arrive(copies)
        total = ring_own[index, own]
        for step in range(1, regions):
            total = total + ring_in[index, step - 1].astype(F32)
        return total

    rows_sent = send_rows(1, proc_asked, mesh_mid)
    everything += rows_sent
    mid_out[...] = mesh_mid
    lefts[4] = to_samples(mid_out, left_in.at[2])
    for index in lefts:
        everything += lefts[index]
    proc_pre = dot_split(p_pick, dot(mesh_mid, proc_send[...])) + dot_split(
        p_recv, dot(mesh_mid, proc_recv[...])
    )
    arrive(rows_sent)
    proc_pre = proc_pre + dot_split(p_far, dot(far_rows(1), proc_send[...]))
    proc_gate = jax.nn.sigmoid(proc_pre)
    proc_act_sum = dot(p_live_t, (proc_pre * proc_gate).astype(BF16))
    shared = {}
    shared[5] = share_factor(5, proc_act_sum)
    proc_dpre = (proc_hidden * (proc_gate * (1.0 + proc_pre * (1.0 - proc_gate)))).astype(BF16)

    def send_terms(graph, far, weights):
        term_out[graph] = times_transposed(far, weights).astype(BF16).reshape(regions, CAP, -1)
        copies = []
        for step in range(1, regions):
            for c_step in range(cores):
                copies.append(
                    send(
                        term_out.at[graph, space_at(step)],
                        term_in.at[graph, core, own],
                        place(space_at(step), sample, core_at(c_step)),
                    )
                )
        return copies

    def returned(graph, asked):
        return left_transposed(
            jnp.concatenate([asked] * cores, axis=0),
            term_in[graph].reshape(cores * slots, -1),
        )

    proc_far = dot(proc_match, proc_dpre).astype(BF16)
    terms = send_terms(1, proc_far, proc_send[...])
    everything += terms
    proc_by_sender = dot(p_pick_t, proc_dpre)
    proc_by_receiver = dot(p_recv_t, proc_dpre)
    part_out[1] = split_dot_transposed(proc_by_receiver, proc_recv[...]) + split_dot_transposed(
        proc_by_sender, proc_send[...]
    )
    swapped = send(part_out.at[1], part_in.at[1], other)
    everything.append(swapped)

    shared[3] = share(
        3,
        left_transposed(mesh_mid, proc_by_sender.astype(BF16))
        + left_transposed(far_rows(1), proc_far),
    )
    shared[4] = share_factor(4, proc_by_receiver)
    part_out[2] = split_dot(proc_act_sum, proc_out[...])
    out_swap = send(part_out.at[2], part_in.at[2], other)
    everything.append(out_swap)
    passed = {}
    passed[5] = pass_on(5, shared[5])

    arrive(terms)
    swapped.wait_recv()
    mesh_mid_grad = cot_block.astype(F32) + (
        (part_out[1] + part_in[1]) + returned(1, proc_asked)
    )

    mid_rounded = mesh_mid_grad.astype(BF16)
    enc_hidden = dot_split(e_live, times_transposed(mid_rounded, enc_out[...]))
    enc_dpre = (enc_hidden * enc_slope).astype(BF16)
    passed[3] = pass_on(3, shared[3])
    shared[2] = share(2, left_transposed(mid_rounded, enc_act_sum.astype(BF16)))
    enc_by_sender = dot(e_pick_t, enc_dpre)
    enc_by_receiver = dot(e_recv_t, enc_dpre)
    enc_far = dot(enc_match, enc_dpre).astype(BF16)
    shared[0] = share(
        0,
        left_transposed(grid_block, enc_by_sender.astype(BF16))
        + left_transposed(far_rows(0), enc_far),
    )
    passed[4] = pass_on(4, shared[4])
    shared[1] = share_factor(1, enc_by_receiver)
    passed[2] = pass_on(2, shared[2])
    terms = send_terms(0, enc_far, enc_send[...])
    everything += terms
    last_out[0:grid_total] = split_dot_transposed(enc_by_sender, enc_send[...])
    last_out[grid_total : grid_total + mesh_total] = split_dot_transposed(
        enc_by_receiver, enc_recv[...]
    )
    last_swap = send(last_out, last_in, other)
    everything.append(last_swap)

    for index in (0, 1):
        passed[index] = pass_on(index, shared[index])
    for index in shared:
        everything += shared[index] + passed[index]

    out_swap.wait_recv()
    mesh_out[...] = (mesh_mid.astype(F32) + (part_out[2] + part_in[2])).astype(BF16)
    arrive(terms)
    last_swap.wait_recv()
    grid_grad[...] = (last_out[0:grid_total] + last_in[0:grid_total]) + returned(0, enc_asked)
    tail = slice(grid_total, grid_total + mesh_total)
    mesh_grad[...] = mesh_mid_grad + (last_out[tail] + last_in[tail])

    g_proc_out[...] = finish(5, passed[5])
    g_proc_send[...] = finish(3, passed[3])
    g_proc_recv[...] = finish(4, passed[4])
    g_enc_out[...] = finish(2, passed[2])
    g_enc_send[...] = finish(0, passed[0])
    g_enc_recv[...] = finish(1, passed[1])
    for copy in everything:
        copy.wait_send()


def place_kernel(*refs):
    sources, targets, sems = refs[:9], refs[9:18], refs[18]
    copies = [
        pltpu.make_async_copy(sources[i], targets[i], sems.at[i]) for i in range(9)
    ]
    for copy in copies:
        copy.start()
    for copy in copies:
        copy.wait()


def fused_body(regions, samples, cores, grid, mesh_nodes, cot, *rest):
    weights = rest[:6]
    given = [grid[0], mesh_nodes[0], cot[0], *weights]
    given += [index.reshape(1, -1) for index in rest[6:]]
    grid_total, width = grid.shape[1:]
    mesh_total = mesh_nodes.shape[1]
    hidden = weights[0].shape[1]
    shard = width // (regions * samples)
    last_total = grid_total + mesh_total
    copies = (regions - 1) * (3 + 2 * cores + 6) + 9 * (samples - 1) + 4
    vmem = pl.BlockSpec(memory_space=pltpu.VMEM)
    outs = pl.pallas_call(
        functools.partial(fused_kernel, regions, samples, cores),
        out_shape=(
            jax.ShapeDtypeStruct((mesh_total, width), BF16),
            jax.ShapeDtypeStruct((grid_total, width), F32),
            jax.ShapeDtypeStruct((mesh_total, width), F32),
            jax.ShapeDtypeStruct((shard, hidden), F32),
            jax.ShapeDtypeStruct((shard, hidden), F32),
            jax.ShapeDtypeStruct((shard, hidden), F32),
            jax.ShapeDtypeStruct((shard, hidden), F32),
            jax.ShapeDtypeStruct((shard, hidden), F32),
            jax.ShapeDtypeStruct((shard, hidden), F32),
        ),
        in_specs=[pl.BlockSpec(memory_space=pl.ANY)] * 15,
        out_specs=(vmem,) * 9,
        scratch_shapes=[pltpu.VMEM(array.shape, array.dtype) for array in given]
        + [
            pltpu.VMEM((regions, 2 * CAP, 128), F32),
            pltpu.VMEM((regions, 2 * CAP, 128), F32),
            pltpu.VMEM((2, regions, CAP, width), BF16),
            pltpu.VMEM((2, regions, CAP, width), BF16),
            pltpu.VMEM((2, regions, CAP, width), BF16),
            pltpu.VMEM((2, cores, regions, CAP, width), BF16),
            pltpu.VMEM((3, mesh_total, width), F32),
            pltpu.VMEM((3, mesh_total, width), F32),
            pltpu.VMEM((last_total, width), F32),
            pltpu.VMEM((last_total, width), F32),
            pltpu.VMEM((6, samples, regions, shard, hidden), F32),
            pltpu.VMEM((6, samples, regions, shard, hidden), BF16),
            pltpu.VMEM((6, samples - 1, regions, shard, hidden), BF16),
            pltpu.VMEM((6, regions, shard, hidden), F32),
            pltpu.VMEM((6, regions, shard, hidden), BF16),
            pltpu.VMEM((6, regions - 1, shard, hidden), BF16),
            pltpu.SemaphoreType.DMA((copies,)),
            pltpu.SemaphoreType.DMA((copies,)),
            pltpu.SemaphoreType.DMA((15,)),
            pltpu.VMEM((mesh_total, width), BF16),
            pltpu.VMEM((3, samples - 1, mesh_total, width), BF16),
            pltpu.VMEM((3, mesh_total, hidden), BF16),
            pltpu.VMEM((3, samples - 1, mesh_total, hidden), BF16),
        ],
        compiler_params=pltpu.CompilerParams(
            collective_id=0, has_side_effects=True, vmem_limit_bytes=58 * 2**20
        ),
    )(*given)
    outs = pl.pallas_call(
        place_kernel,
        out_shape=[jax.ShapeDtypeStruct(out.shape, out.dtype) for out in outs],
        in_specs=[vmem] * 9,
        out_specs=[pl.BlockSpec(memory_space=pl.ANY)] * 9,
        scratch_shapes=[pltpu.SemaphoreType.DMA((9,))],
    )(*outs)
    gradients = [out.T if i in (2, 5) else out for i, out in enumerate(outs[3:])]
    return (outs[0][None], outs[1][None], outs[2][None], *gradients)


def chosen_body(mesh):
    regions, samples, cores = (mesh.shape[name] for name in ("space", "dp", "chan"))
    shards = regions * samples

    def run(*args):
        width = args[0].shape[2]
        if regions > 16 or samples < 2 or cores != 2 or width % (16 * shards):
            return body(*args)
        return fused_body(regions, samples, cores, *args)

    return run


def solution(mesh):
    placed = (
        P(("groups", "dp"), "space", None),
        P(("groups", "dp"), "space", None),
        P(("groups", "dp"), "space", None),
        P(None, "chan"),
        P(None, "chan"),
        P("chan", None),
        P(None, "chan"),
        P(None, "chan"),
        P("chan", None),
        P("space"),
        P("space"),
        P("space"),
        P("space"),
        P("space"),
        P("space"),
    )
    return jax.shard_map(
        chosen_body(mesh),
        mesh=mesh,
        in_specs=placed,
        out_specs=(
            P(("groups", "dp"), "space", None),
            P(("groups", "dp"), "space", None),
            P(("groups", "dp"), "space", None),
            P(("groups", "space", "dp"), "chan"),
            P(("groups", "space", "dp"), "chan"),
            P(("groups", "chan"), ("space", "dp")),
            P(("groups", "space", "dp"), "chan"),
            P(("groups", "space", "dp"), "chan"),
            P(("groups", "chan"), ("space", "dp")),
        ),
        check_vma=False,
    )
```
